32 devices in a mesh: sub: 8 (over z, x), blk: 4 (over y, core).
Axes of the slice: x: 2, y: 2, z: 4, core: 2. Of those that a mesh axis runs over, the one named last changes fastest.
Arguments:
- factor: bfloat16 [16, 2048, 2048], P('sub', None, 'blk'), may hold values from -0.125 to 0.125
- samples: bfloat16 [16, 2048, 128], P('sub', 'blk'), may hold values from -6 to 6
- diagonal: bfloat16 [16, 128, 16], P('sub'), may hold values from 0.25 to 1
- coupling: bfloat16 [16, 64, 2048], P('sub', 'blk'), may hold values from -0.125 to 0.125
- blocks: int32 [16], P('sub'), may hold values from 80 to 128, as said below
- peer_device: int32 [16, 128], P('sub'), may hold values from 0 to 7, as said below
- peer_lane: int32 [16, 128], P('sub'), may hold values from 0 to 34, as said below
- owns_face: int32 [16, 128], P('sub'), may hold values from 0 to 1, as said below
Outputs:
- interior: bfloat16 [16, 64, 128], P('sub', 'blk')
The draws below stay inside these ranges and needn't reach their ends.
Inputs may be any that keep to these rules, and one draw needn't show every extreme that they name: Each subdomain's interface has blocks face blocks; over the subdomains of one index of sub they sum to 208. `peer_device`: live slots are matched in pairs of partners as the statement says, one owning side each; each index of sub owns 104 faces and holds 104 faces owned elsewhere; all faces between two indices of sub are owned by the same one of them; slots that are not live hold 0. Live slots of one index of sub with the same peer_device and the same owns_face have different peer_lane; slots that are not live hold 0. `owns_face`: slots that are not live hold 0.
All inputs are finite; a program needn't handle non-finite values.
Results may differ from the reference program's by a relative error of at most 0.013.
Values may be sent and summed in bfloat16 or wider, within the bound.
A program may use at most 64 MiB of HBM per device.

```python
import math
import jax
import jax.numpy as jnp
from jax import lax

TILE = 16
MAXB = 128
SUB_DEV = 2
NI = 64
MIDB = 104
ORDER = 2048
COLS = 128
SUBS = 16
FACE_HALF = 104
HALF_CYCLE = 3
CAP = 35
N_SUB = 8
N_BLK = 4


def face_plan(key):
    folded = jax.random.fold_in(key, 29)
    subkeys = jax.random.split(folded, 5)
    placing = jax.random.permutation(subkeys[0], N_SUB).astype(jnp.int32)
    position = jnp.zeros((N_SUB,), jnp.int32).at[placing].set(jnp.arange(N_SUB, dtype=jnp.int32))
    spread_most = MAXB - MIDB
    pair_count = SUB_DEV // 2
    spreads = jax.random.randint(subkeys[1], (N_SUB, pair_count), 0, spread_most + 1).astype(jnp.int32)
    forced = jax.random.randint(subkeys[2], (), 0, N_SUB)
    spreads = spreads.at[forced, 0].set(spread_most)
    shifts = jnp.zeros((N_SUB, SUB_DEV), jnp.int32)
    shifts = shifts.at[:, 0:2 * pair_count:2].set(spreads)
    shifts = shifts.at[:, 1:2 * pair_count:2].set(-spreads)
    orders = jax.vmap(lambda subkey: jax.random.permutation(subkey, SUB_DEV))(jax.random.split(subkeys[3], N_SUB)).astype(jnp.int32)
    shifts = jnp.take_along_axis(shifts, orders, axis=1)
    counts = MIDB + shifts
    end_order = jax.vmap(lambda subkey: jax.random.permutation(subkey, 2 * FACE_HALF))(jax.random.split(subkeys[4], N_SUB)).astype(jnp.int32)
    starts = jnp.cumsum(counts, axis=1) - counts
    slot_index = jnp.arange(MAXB, dtype=jnp.int32)
    ordinal = starts[:, :, None] + slot_index[None, None, :]
    live_slot = slot_index[None, None, :] < counts[:, :, None]
    ordinal = jnp.minimum(ordinal, 2 * FACE_HALF - 1)
    face_end = jnp.take_along_axis(end_order, ordinal.reshape(N_SUB, SUB_DEV * MAXB), axis=1).reshape(N_SUB, SUB_DEV, MAXB)
    owned_end = face_end < FACE_HALF
    face_number = jnp.where(owned_end, face_end, face_end - FACE_HALF)
    cycle_offset = 1 + face_number % HALF_CYCLE
    lane_index = face_number // HALF_CYCLE
    cycle_step = jnp.where(owned_end, cycle_offset, -cycle_offset)
    target = (position[:, None, None] + cycle_step) % N_SUB
    peer_found = placing[target]
    peer_found = jnp.where(live_slot, peer_found, jnp.zeros_like(peer_found)).reshape(SUBS, MAXB).astype(jnp.int32)
    lane_index = jnp.where(live_slot, lane_index, jnp.zeros_like(lane_index)).reshape(SUBS, MAXB).astype(jnp.int32)
    owner_flag = jnp.where(live_slot & owned_end, 1, 0).reshape(SUBS, MAXB).astype(jnp.int32)
    return (counts.reshape(SUBS).astype(jnp.int32), peer_found, lane_index, owner_flag)


def draw_blocks(key, part):
    return face_plan(key)[0]


def draw_peer_device(key, part):
    return face_plan(key)[1]


def draw_peer_lane(key, part):
    return face_plan(key)[2]


def draw_owns_face(key, part):
    return face_plan(key)[3]


def shard_levels(key, dims, shards, least, high):
    factor_of, own = 1.0, jax.random.fold_in(key, 6)
    for dim, shards_of in shards:
        draws = jnp.exp(jax.random.uniform(jax.random.fold_in(own, dim), (shards_of,), jnp.float32, least / len(shards), high / len(shards)))
        factor_of = factor_of * jnp.repeat(draws, dims[dim] // shards_of).reshape([-1 if axis == dim else 1 for axis in range(len(dims))])
    return factor_of


def centred(key, dims, width, limit, shards=(), kind=jnp.bfloat16):
    factor_of = shard_levels(key, dims, shards, -0.22, 0.18) if shards else 1.0
    values = jax.random.normal(key, dims, jnp.float32) * width * factor_of
    return jnp.minimum(jnp.maximum(values, -limit), limit).astype(kind)


def setup_inputs(seed: int = 0) -> dict:
    seeds = jax.random.split(jax.random.key(seed), 9)
    factor = centred(seeds[0], (SUBS, ORDER, ORDER), ORDER ** -0.5, 0.125, ((0, 8), (2, 4)))
    samples = centred(seeds[1], (SUBS, ORDER, COLS), 1.0, 6.0, ((0, 8), (1, 4)))
    diagonal = jnp.clip(jnp.exp(math.log(1.0) - 1.3862944 * jax.random.uniform(seeds[2], (SUBS, MAXB, TILE), jnp.float32) ** shard_levels(seeds[2], (SUBS, MAXB, TILE), ((0, 8),), -0.2, 0.2)), 0.25, 1.0).astype(jnp.bfloat16)
    coupling = centred(seeds[3], (SUBS, NI, ORDER), ORDER ** -0.5, 0.125, ((0, 8), (1, 4)))
    blocks = draw_blocks(jax.random.fold_in(seeds[8], 71), 0)
    peer_device = draw_peer_device(jax.random.fold_in(seeds[8], 71), 0)
    peer_lane = draw_peer_lane(jax.random.fold_in(seeds[8], 71), 0)
    owns_face = draw_owns_face(jax.random.fold_in(seeds[8], 71), 0)
    return dict(factor=factor, samples=samples, diagonal=diagonal, coupling=coupling, blocks=blocks, peer_device=peer_device, peer_lane=peer_lane, owns_face=owns_face)


def apply_factor(operands):
    factor_one, sample_one, count_one = operands
    row_index = jnp.arange(ORDER, dtype=jnp.int32)
    live_rows = row_index < count_one * TILE
    driven = jnp.where(live_rows[:, None], sample_one, jnp.zeros_like(sample_one))
    factor_wide = factor_one.astype(jnp.float32)
    reduced = jnp.dot(factor_wide.T, driven.astype(jnp.float32), preferred_element_type=jnp.float32, precision=lax.Precision.HIGHEST).astype(jnp.bfloat16)
    reduced = jnp.where(live_rows[:, None], reduced, jnp.zeros_like(reduced))
    quarter = ORDER // N_BLK
    running = jnp.zeros((ORDER, COLS), jnp.float32)
    for piece_index in range(N_BLK):
        lower = piece_index * quarter
        product = jnp.dot(factor_wide[:, lower:lower + quarter], reduced[lower:lower + quarter].astype(jnp.float32), preferred_element_type=jnp.float32, precision=lax.Precision.HIGHEST)
        rounded = lax.optimization_barrier(product.astype(jnp.bfloat16))
        running = running + rounded.astype(jnp.float32)
    return running.astype(jnp.bfloat16)


def recover(operands):
    coupling_one, coef_one = operands
    product = jnp.dot(coupling_one.astype(jnp.float32), coef_one.astype(jnp.float32), preferred_element_type=jnp.float32, precision=lax.Precision.HIGHEST)
    return product.astype(jnp.bfloat16)


def reference(factor, samples, diagonal, coupling, blocks, peer_device, peer_lane, owns_face):
    traces = lax.map(apply_factor, (factor, samples, blocks))
    slot_total = SUBS * MAXB
    slot_traces = traces.reshape(slot_total, TILE, COLS).astype(jnp.float32)
    slot_diag = diagonal.reshape(slot_total, TILE).astype(jnp.float32)
    slot_index = jnp.arange(slot_total, dtype=jnp.int32)
    device_of = (slot_index // MAXB) // SUB_DEV
    position = slot_index % MAXB
    live_slot = position < jnp.repeat(blocks, MAXB)
    peers = peer_device.reshape(-1)
    lanes = peer_lane.reshape(-1)
    owning = owns_face.reshape(-1)
    table_size = N_SUB * N_SUB * CAP * 2
    own_key = ((device_of * N_SUB + peers) * CAP + lanes) * 2 + owning
    own_key = jnp.where(live_slot, own_key, table_size)
    table = jnp.zeros((table_size + 1,), jnp.int32).at[own_key].set(slot_index)
    wanted = ((peers * N_SUB + device_of) * CAP + lanes) * 2 + (1 - owning)
    wanted = jnp.where(live_slot, wanted, table_size)
    partner = table[wanted]
    summed = slot_traces + slot_traces[partner]
    divisor = slot_diag + slot_diag[partner]
    coef = (summed / divisor[:, :, None]).astype(jnp.bfloat16)
    coef = jnp.where(live_slot[:, None, None], coef, jnp.zeros_like(coef))
    coefficients = coef.reshape(SUBS, ORDER, COLS)
    return lax.map(recover, (coupling, coefficients))
```

```python
import functools

import jax
import jax.numpy as jnp
from jax import lax
from jax.experimental import pallas as pl
from jax.experimental.pallas import tpu as pltpu
from jax.sharding import PartitionSpec as P

FACE_HALF = 104
MESH = pl.DeviceIdType.MESH
F32, BF16 = jnp.float32, jnp.bfloat16


def kernel(
    n_sub, n_blk, pad,
    factor, samples, diagonal, coupling, blocks, peer_device, peer_lane, out,
    fac, drv, tr, parts, near, far, mixed, kept, place, face_out, face_in,
    coup_t, coup_out, coup_in, inner, inner_in, diag_pad,
    local_sem, near_sem, far_sem, relay_sem, near_sum, far_sum, face_sem, coup_sem, last_sem,
):
    me, here = lax.axis_index("sub"), lax.axis_index("blk")
    subs, order, quarter = fac.shape
    slots_one, tile = diagonal.shape[1], diagonal.shape[2]
    slots = subs * slots_one
    cols = samples.shape[2]
    mine = tile // n_blk
    inner_rows = coupling.shape[1]
    twin = here + 1 - 2 * lax.rem(here, 2)
    cross = lax.rem(here + 2, n_blk)
    diag = lax.rem(twin + 2, n_blk)

    def remote(src, dst, sems, where):
        return pltpu.make_async_remote_copy(
            src_ref=src, dst_ref=dst, send_sem=sems.at[0], recv_sem=sems.at[1],
            device_id=where, device_id_type=MESH,
        )

    def sub_peer(step):
        return lax.rem(me + step, n_sub)

    load = []
    for s in range(subs):
        one = pltpu.make_async_copy(factor.at[s], fac.at[s], local_sem.at[s])
        one.start()
        load.append(one)
    own = pltpu.make_async_copy(samples, drv.at[here], local_sem.at[subs])
    own.start()

    barrier = pltpu.get_barrier_semaphore()
    for b in (twin, cross, diag):
        pl.semaphore_signal(barrier, inc=1, device_id={"blk": b}, device_id_type=MESH)

    def greet(step, carry):
        pl.semaphore_signal(
            barrier, inc=1, device_id={"sub": sub_peer(step)}, device_id_type=MESH
        )
        return carry

    lax.fori_loop(1, n_sub, greet, 0)
    pl.semaphore_wait(barrier, n_sub - 1 + 3)

    to_far = [
        remote(samples.at[s], drv.at[here, s], far_sem.at[s], {"blk": cross}) for s in range(subs)
    ]
    to_near = [
        remote(samples.at[s], drv.at[here, s], near_sem.at[s], {"blk": twin}) for s in range(subs)
    ]
    for s in range(subs):
        to_far[s].start()
    for s in range(subs):
        to_near[s].start()

    rows = n_sub * pad
    slot_of = lax.broadcasted_iota(jnp.int32, (1, slots_one), 1)
    columns = []
    for s in range(subs):
        row = peer_device[pl.ds(s, 1), :] * pad + peer_lane[pl.ds(s, 1), :]
        row = jnp.where(slot_of < blocks[s], row, -1)
        row_of = lax.broadcasted_iota(jnp.int32, (rows, slots_one), 0)
        place[:, s * slots_one:(s + 1) * slots_one] = jnp.where(row_of == row, 1.0, 0.0).astype(BF16)
        columns.append(jnp.broadcast_to(row.astype(F32), (slots_one, slots_one)).T[:, :1])
    column = jnp.concatenate(columns, axis=0).astype(jnp.int32)
    live = column >= 0
    inside = (column >= me * pad) & (column < me * pad + pad)
    lane_of = lax.broadcasted_iota(jnp.int32, (slots, rows), 1)
    collect = jnp.where(lane_of == column, 1.0, 0.0).astype(BF16)
    self_rows = pl.ds(pl.multiple_of(me * pad, 16), pad)

    def face_copy(k, step):
        there = pl.ds(pl.multiple_of(sub_peer(step) * pad, 16), pad)
        return remote(
            face_out.at[k, there], face_in.at[k, self_rows], face_sem.at[k], {"sub": sub_peer(step)}
        )

    def send_faces(k, value):
        face_out[k] = jnp.dot(place[...], value, preferred_element_type=F32).astype(BF16)
        face_in[k, self_rows, :] = face_out[k, self_rows, :]

        def go(step, carry):
            face_copy(k, step).start()
            return carry

        lax.fori_loop(1, n_sub, go, 0)

    def faces(k, value):
        all_rows = pl.ds(0, (n_sub - 1) * pad)
        remote(
            face_out.at[k, all_rows], face_in.at[k, all_rows], face_sem.at[k], {"sub": sub_peer(1)}
        ).wait()
        got = jnp.dot(collect, face_in[k], preferred_element_type=F32)
        return jnp.where(inside, 0.0, value.astype(F32)) + got

    diag_pad[...] = jnp.zeros_like(diag_pad)
    diag_pad[:, :tile] = diagonal[...].reshape(slots, tile)
    send_faces(mine, diag_pad[...])

    wide = coupling[...].reshape(subs * inner_rows, order).astype(F32)
    filler = jnp.zeros((coup_t.shape[1] - subs * inner_rows, order), F32)
    coup_t[...] = jnp.concatenate([wide, filler], axis=0).T
    for t in range(tile):
        piece = coup_t[pl.ds(t, slots_one, stride=tile), :].T
        coup_out[t] = piece[:subs * inner_rows].astype(BF16)
    coup_in[here] = coup_out[pl.ds(here * mine, mine)]
    coup_copies = [
        remote(coup_out.at[pl.ds(b * mine, mine)], coup_in.at[here], coup_sem.at[i], {"blk": b})
        for i, b in enumerate((twin, cross, diag))
    ]
    for c in coup_copies:
        c.start()

    own.wait()
    relays = []
    row_in = lax.broadcasted_iota(jnp.int32, (quarter, 1), 0)
    lane_in = lax.broadcasted_iota(jnp.int32, (1, quarter), 1)

    def first(s, b):
        begin = pl.multiple_of(b * quarter, quarter)
        rows_live = row_in + begin < blocks[s] * tile
        value = drv[b, s]
        value = jnp.where(rows_live, value, jnp.zeros_like(value))
        return lax.dot_general(
            value, fac[s, pl.ds(begin, quarter), :], (((0,), (0,)), ((), ())),
            preferred_element_type=F32,
        )

    for s in range(subs):
        load[s].wait()
        reduced = first(s, here)
        to_near[s].wait()
        reduced += first(s, twin)
        to_far[s].wait()
        relay = remote(drv.at[cross, s], drv.at[cross, s], relay_sem.at[s], {"blk": twin})
        relay.start()
        reduced += first(s, cross)
        relay.wait()
        reduced += first(s, diag)
        alive = lane_in + here * quarter < blocks[s] * tile
        reduced = jnp.where(alive, reduced, 0.0).astype(BF16)
        for q in range(0, order, quarter):
            tr[s, q:q + quarter, :] = lax.dot_general(
                fac[s, q:q + quarter, :], reduced, (((1,), (1,)), ((), ())),
                preferred_element_type=F32,
            )
        for t in range(tile):
            parts[t, s * slots_one:(s + 1) * slots_one, :] = tr[
                s, pl.ds(t, slots_one, stride=tile), :
            ].astype(BF16)

    near_copies = []
    for k in range(mine):
        pair = [
            remote(parts.at[diag * mine + k], near.at[k, 1], near_sum.at[k, 1], {"blk": twin}),
            remote(parts.at[twin * mine + k], near.at[k, 0], near_sum.at[k, 0], {"blk": twin}),
        ]
        for c in pair:
            c.start()
        near_copies.append(pair)
    far_copies = []
    for k in range(mine):
        near_copies[k][0].wait()
        mixed[k] = (parts[cross * mine + k].astype(F32) + near[k, 1].astype(F32)).astype(BF16)
        c = remote(mixed.at[k], far.at[k], far_sum.at[k], {"blk": cross})
        c.start()
        far_copies.append(c)
    for k in range(mine):
        near_copies[k][1].wait()
        far_copies[k].wait()
        kept[k] = (
            parts[here * mine + k].astype(F32) + near[k, 0].astype(F32) + far[k].astype(F32)
        ).astype(BF16)
        send_faces(k, kept[k])

    for c in coup_copies:
        c.wait()
    divisors = faces(mine, diag_pad[...])
    lane_t = lax.broadcasted_iota(jnp.int32, (slots, cols), 1)
    sums = [None] * subs
    for k in range(mine):
        divisor = jnp.sum(
            jnp.where(lane_t == here * mine + k, divisors, 0.0), axis=1, keepdims=True
        )
        divisor = jnp.where(live, divisor, 1.0)
        coef = jnp.where(live, faces(k, kept[k]) / divisor, 0.0).astype(BF16)
        for s in range(subs):
            left = coup_in[:, k, s * inner_rows:(s + 1) * inner_rows, :]
            got = jnp.dot(
                left.reshape(n_blk * inner_rows, slots_one),
                coef[s * slots_one:(s + 1) * slots_one],
                preferred_element_type=F32,
            )
            sums[s] = got if k == 0 else sums[s] + got
    for s in range(subs):
        inner[:, s] = sums[s].reshape(n_blk, inner_rows, cols)
    last = [
        remote(inner.at[b], inner_in.at[here], last_sem.at[i], {"blk": b})
        for i, b in enumerate((twin, cross, diag))
    ]
    for c in last:
        c.start()
    total = inner[here]
    for c in last:
        c.wait()
    for b in (twin, cross, diag):
        total = total + inner_in[b]
    out[...] = total.astype(BF16)


def local(factor, samples, diagonal, coupling, blocks, peer_device, peer_lane, owns_face):
    n_sub, n_blk = lax.axis_size("sub"), lax.axis_size("blk")
    subs, order, quarter = factor.shape
    slots_one, tile = diagonal.shape[1], diagonal.shape[2]
    slots, cols = subs * slots_one, samples.shape[2]
    mine, inner_rows = tile // n_blk, coupling.shape[1]
    half_cycle = (n_sub - 1) // 2
    capacity = (FACE_HALF + half_cycle - 1) // half_cycle
    pad = -(-capacity // 16) * 16
    rows = n_sub * pad
    flops = 4 * subs * order * quarter * cols
    vmem, hbm = pl.BlockSpec(memory_space=pltpu.VMEM), pl.BlockSpec(memory_space=pl.ANY)
    smem = pl.BlockSpec(memory_space=pltpu.SMEM)
    sem = pltpu.SemaphoreType.DMA
    coup_lanes = -(-subs * inner_rows // 128) * 128
    return pl.pallas_call(
        functools.partial(kernel, n_sub, n_blk, pad),
        out_shape=jax.ShapeDtypeStruct((subs, inner_rows, cols), BF16),
        in_specs=[hbm, hbm, vmem, vmem, smem, vmem, vmem],
        out_specs=vmem,
        scratch_shapes=[
            pltpu.VMEM((subs, order, quarter), BF16),
            pltpu.VMEM((n_blk, subs, quarter, cols), BF16),
            pltpu.VMEM((subs, order, cols), F32),
            pltpu.VMEM((tile, slots, cols), BF16),
            pltpu.VMEM((mine, 2, slots, cols), BF16),
            pltpu.VMEM((mine, slots, cols), BF16),
            pltpu.VMEM((mine, slots, cols), BF16),
            pltpu.VMEM((mine, slots, cols), BF16),
            pltpu.VMEM((rows, slots), BF16),
            pltpu.VMEM((mine + 1, rows, cols), BF16),
            pltpu.VMEM((mine + 1, rows, cols), BF16),
            pltpu.VMEM((order, coup_lanes), F32),
            pltpu.VMEM((tile, subs * inner_rows, slots_one), BF16),
            pltpu.VMEM((n_blk, mine, subs * inner_rows, slots_one), BF16),
            pltpu.VMEM((n_blk, subs, inner_rows, cols), F32),
            pltpu.VMEM((n_blk, subs, inner_rows, cols), F32),
            pltpu.VMEM((slots, cols), BF16),
            sem((subs + 1,)),
            sem((subs, 2)),
            sem((subs, 2)),
            sem((subs, 2)),
            sem((mine, 2, 2)),
            sem((mine, 2)),
            sem((mine + 1, 2)),
            sem((3, 2)),
            sem((3, 2)),
        ],
        compiler_params=pltpu.CompilerParams(
            collective_id=0, has_side_effects=True, vmem_limit_bytes=48 * 1024 * 1024
        ),
        cost_estimate=pl.CostEstimate(
            flops=flops, bytes_accessed=2 * factor.size, transcendentals=0
        ),
    )(factor, samples, diagonal, coupling, blocks, peer_device, peer_lane)


def solution(mesh):
    placed = (
        P("sub", None, "blk"),
        P("sub", "blk", None),
        P("sub", None, None),
        P("sub", "blk", None),
        P("sub"),
        P("sub", None),
        P("sub", None),
        P("sub", None),
    )
    return jax.shard_map(
        local, mesh=mesh, in_specs=placed, out_specs=P("sub", "blk", None), check_vma=False
    )
```

```python
import functools

import jax
import jax.numpy as jnp
from jax import lax
from jax.experimental import pallas as pl
from jax.experimental.pallas import tpu as pltpu
from jax.sharding import PartitionSpec as P

FACE_HALF = 104
MESH = pl.DeviceIdType.MESH
F32, BF16 = jnp.float32, jnp.bfloat16


def kernel(
    n_sub, n_blk, pad, main, extra,
    factor, samples, diagonal, coupling, blocks_in, peer_in, lane_in_ref, out,
    fac, drv, tr, parts, near, far, mixed, kept, diag_out, diag_in, main_out, main_in,
    tail_out, tail_in, coup_t, coup_out, coup_in, inner, inner_in, diag_own,
    diag_raw, coup, peer_device, peer_lane, blocks,
    local_sem, small_sem, near_sem, far_sem, relay_sem, near_sum, far_sum, diag_sem, main_sem,
    tail_sem, coup_sem, last_sem,
):
    me, here = lax.axis_index("sub"), lax.axis_index("blk")
    subs, order, quarter = fac.shape
    tile, slots_one = diagonal.shape[1], diagonal.shape[2]
    slots = subs * slots_one
    cols = samples.shape[2]
    mine = tile // n_blk
    inner_rows = coupling.shape[1]
    twin = here + 1 - 2 * lax.rem(here, 2)
    cross = lax.rem(here + 2, n_blk)
    diag = lax.rem(twin + 2, n_blk)

    def remote(src, dst, sems, where):
        return pltpu.make_async_remote_copy(
            src_ref=src, dst_ref=dst, send_sem=sems.at[0], recv_sem=sems.at[1],
            device_id=where, device_id_type=MESH,
        )

    def sub_peer(step):
        return lax.rem(me + step, n_sub)

    barrier = pltpu.get_barrier_semaphore()
    for b in (twin, cross, diag):
        pl.semaphore_signal(barrier, inc=1, device_id={"blk": b}, device_id_type=MESH)

    def greet(step, carry):
        pl.semaphore_signal(
            barrier, inc=1, device_id={"sub": sub_peer(step)}, device_id_type=MESH
        )
        return carry

    lax.fori_loop(1, n_sub, greet, 0)

    small = [
        pltpu.make_async_copy(src, dst, small_sem.at[i])
        for i, (src, dst) in enumerate((
            (blocks_in, blocks), (peer_in, peer_device), (lane_in_ref, peer_lane),
            (diagonal, diag_raw), (coupling, coup),
        ))
    ]
    for c in small:
        c.start()
    own = pltpu.make_async_copy(samples, drv.at[here], local_sem.at[subs])
    own.start()
    load = []
    for s in range(subs):
        one = pltpu.make_async_copy(factor.at[s], fac.at[s], local_sem.at[s])
        one.start()
        load.append(one)

    pl.semaphore_wait(barrier, n_sub - 1 + 3)

    to_far = [
        remote(samples.at[s], drv.at[here, s], far_sem.at[s], {"blk": cross}) for s in range(subs)
    ]
    to_near = [
        remote(samples.at[s], drv.at[here, s], near_sem.at[s], {"blk": twin}) for s in range(subs)
    ]
    for s in range(subs):
        to_far[s].start()
    for s in range(subs):
        to_near[s].start()

    for c in small:
        c.wait()
    slot_of = lax.broadcasted_iota(jnp.int32, (1, slots_one), 1)
    peer_rows, peer_cols, lane_cols = [], [], []
    for s in range(subs):
        peer = jnp.where(slot_of < blocks[s], peer_device[pl.ds(s, 1), :], -1)
        peer_rows.append(peer)
        square = (slots_one, slots_one)
        peer_cols.append(jnp.broadcast_to(peer.astype(F32), square).T[:, :1])
        lanes = peer_lane[pl.ds(s, 1), :].astype(F32)
        lane_cols.append(jnp.broadcast_to(lanes, square).T[:, :1])
    peer_row = jnp.concatenate(peer_rows, axis=1)
    lane_row = jnp.concatenate([peer_lane[pl.ds(s, 1), :] for s in range(subs)], axis=1)
    peer_col = jnp.concatenate(peer_cols, axis=0).astype(jnp.int32)
    lane_col = jnp.concatenate(lane_cols, axis=0).astype(jnp.int32)
    live = peer_col >= 0
    inside = peer_col == me

    def target(peer, lane, size, low, high, offset):
        chosen = (peer >= 0) & (lane >= low) & (lane < high)
        return jnp.where(chosen, peer * size + (lane - low) + offset, -1)

    def place(size, low, high, offset=0):
        row_of = lax.broadcasted_iota(jnp.int32, (n_sub * size, slots), 0)
        wanted = target(peer_row, lane_row, size, low, high, offset)
        return jnp.where(row_of == wanted, 1.0, 0.0).astype(BF16)

    def collect(size, low, high, offset=0):
        lane_of = lax.broadcasted_iota(jnp.int32, (slots, n_sub * size), 1)
        wanted = target(peer_col, lane_col, size, low, high, offset)
        return jnp.where(lane_of == wanted, 1.0, 0.0).astype(BF16)

    def rows_of(index, size):
        return pl.ds(pl.multiple_of(index * size, 16), size)

    def send_faces(value, sent, got, sems, size):
        sent[...] = value.astype(BF16)
        got[rows_of(me, size), :] = sent[rows_of(me, size), :]

        def go(step, carry):
            remote(
                sent.at[rows_of(sub_peer(step), size)], got.at[rows_of(me, size)], sems,
                {"sub": sub_peer(step)},
            ).start()
            return carry

        lax.fori_loop(1, n_sub, go, 0)

    def wait_faces(sent, got, sems, size):
        every = pl.ds(0, (n_sub - 1) * size)
        remote(sent.at[every], got.at[every], sems, {"sub": sub_peer(1)}).wait()

    def dot(left, right):
        return jnp.dot(left, right, preferred_element_type=F32)

    for s in range(subs):
        wide = jnp.concatenate(
            [diag_raw[s].astype(F32), jnp.zeros((cols - tile, slots_one), F32)], axis=0
        )
        diag_own[s * slots_one:(s + 1) * slots_one, :] = wide.T.astype(BF16)
    send_faces(dot(place(pad, 0, pad), diag_own[...]), diag_out, diag_in, diag_sem, pad)

    own.wait()
    row_in = lax.broadcasted_iota(jnp.int32, (quarter, 1), 0)
    lane_in = lax.broadcasted_iota(jnp.int32, (1, quarter), 1)

    def first(s, b):
        begin = pl.multiple_of(b * quarter, quarter)
        rows_live = row_in + begin < blocks[s] * tile
        value = drv[b, s]
        value = jnp.where(rows_live, value, jnp.zeros_like(value))
        return lax.dot_general(
            value, fac[s, pl.ds(begin, quarter), :], (((0,), (0,)), ((), ())),
            preferred_element_type=F32,
        )

    near_copies, far_copies = {}, {}

    def send_near(s):
        span = pl.ds(s * slots_one, slots_one)
        for j, group in ((1, diag), (0, twin)):
            for k in range(mine):
                c = remote(
                    parts.at[group * mine + k, span], near.at[k, j, span],
                    near_sum.at[s, k, j], {"blk": twin},
                )
                c.start()
                near_copies[s, k, j] = c

    def send_far(s):
        span = pl.ds(s * slots_one, slots_one)
        for k in range(mine):
            near_copies[s, k, 1].wait()
            mixed[k, span, :] = (
                parts[cross * mine + k, span, :].astype(F32) + near[k, 1, span, :].astype(F32)
            ).astype(BF16)
            c = remote(mixed.at[k, span], far.at[k, span], far_sum.at[s, k], {"blk": cross})
            c.start()
            far_copies[s, k] = c

    for s in range(subs):
        load[s].wait()
        reduced = first(s, here)
        to_near[s].wait()
        reduced += first(s, twin)
        to_far[s].wait()
        relay = remote(drv.at[cross, s], drv.at[cross, s], relay_sem.at[s], {"blk": twin})
        relay.start()
        reduced += first(s, cross)
        if s:
            send_far(s - 1)
        relay.wait()
        reduced += first(s, diag)
        alive = lane_in + here * quarter < blocks[s] * tile
        reduced = jnp.where(alive, reduced, 0.0).astype(BF16)
        for q in range(0, order, quarter):
            tr[s, q:q + quarter, :] = lax.dot_general(
                fac[s, q:q + quarter, :], reduced, (((1,), (1,)), ((), ())),
                preferred_element_type=F32,
            )
        for t in range(tile):
            parts[t, s * slots_one:(s + 1) * slots_one, :] = tr[
                s, pl.ds(t, slots_one, stride=tile), :
            ].astype(BF16)
        send_near(s)
    send_far(subs - 1)

    tail = None
    for k in range(mine):
        for s in range(subs):
            near_copies[s, k, 0].wait()
            far_copies[s, k].wait()
        kept[k] = (
            parts[here * mine + k].astype(F32) + near[k, 0].astype(F32) + far[k].astype(F32)
        ).astype(BF16)
        if main:
            send_faces(
                dot(place(main, 0, main), kept[k]), main_out.at[k], main_in.at[k], main_sem.at[k],
                main,
            )
        if extra:
            got = dot(place(extra, main, pad, k * (extra // mine)), kept[k])
            tail = got if k == 0 else tail + got
    if extra:
        send_faces(tail, tail_out, tail_in, tail_sem, extra)

    wide = coup[...].reshape(subs * inner_rows, order).astype(F32)
    filler = jnp.zeros((coup_t.shape[1] - subs * inner_rows, order), F32)
    coup_t[...] = jnp.concatenate([wide, filler], axis=0).T
    for t in range(tile):
        piece = coup_t[pl.ds(t, slots_one, stride=tile), :].T
        coup_out[t] = piece[:subs * inner_rows].astype(BF16)
    coup_in[here] = coup_out[pl.ds(here * mine, mine)]
    coup_copies = [
        remote(coup_out.at[pl.ds(b * mine, mine)], coup_in.at[here], coup_sem.at[i], {"blk": b})
        for i, b in enumerate((twin, cross, diag))
    ]
    for c in coup_copies:
        c.start()

    def own_side(value):
        return jnp.where(inside, 0.0, value.astype(F32))

    wait_faces(diag_out, diag_in, diag_sem, pad)
    divisors = own_side(diag_own[...]) + dot(collect(pad, 0, pad), diag_in[...])
    lane_t = lax.broadcasted_iota(jnp.int32, (slots, cols), 1)
    divisor = []
    for k in range(mine):
        one = jnp.sum(jnp.where(lane_t == here * mine + k, divisors, 0.0), axis=1, keepdims=True)
        divisor.append(jnp.where(live, one, 1.0))
    for c in coup_copies:
        c.wait()
    total = []
    for k in range(mine):
        both = own_side(kept[k])
        if main:
            wait_faces(main_out.at[k], main_in.at[k], main_sem.at[k], main)
            both += dot(collect(main, 0, main), main_in[k])
        total.append(both)
    if extra:
        wait_faces(tail_out, tail_in, tail_sem, extra)
        for k in range(mine):
            total[k] += dot(collect(extra, main, pad, k * (extra // mine)), tail_in[...])
    sums = [None] * subs
    for k in range(mine):
        coef = jnp.where(live, total[k] / divisor[k], 0.0).astype(BF16)
        for s in range(subs):
            left = coup_in[:, k, s * inner_rows:(s + 1) * inner_rows, :]
            got = dot(
                left.reshape(n_blk * inner_rows, slots_one),
                coef[s * slots_one:(s + 1) * slots_one],
            )
            sums[s] = got if k == 0 else sums[s] + got
    for s in range(subs):
        inner[:, s] = sums[s].reshape(n_blk, inner_rows, cols)
    last = [
        remote(inner.at[b], inner_in.at[here], last_sem.at[i], {"blk": b})
        for i, b in enumerate((twin, cross, diag))
    ]
    for c in last:
        c.start()
    result = inner[here]
    for c in last:
        c.wait()
    for b in (twin, cross, diag):
        result = result + inner_in[b]
    out[...] = result.astype(BF16)


def local(factor, samples, diagonal, coupling, blocks, peer_device, peer_lane, owns_face):
    n_sub, n_blk = lax.axis_size("sub"), lax.axis_size("blk")
    subs, order, quarter = factor.shape
    slots_one, tile = diagonal.shape[1], diagonal.shape[2]
    slots, cols = subs * slots_one, samples.shape[2]
    mine, inner_rows = tile // n_blk, coupling.shape[1]
    half_cycle = (n_sub - 1) // 2
    capacity = (FACE_HALF + half_cycle - 1) // half_cycle
    pad = -(-capacity // 16) * 16
    main = capacity // 16 * 16
    extra = -(-(capacity - main) * mine // 16) * 16
    flops = 4 * subs * order * quarter * cols
    hbm = pl.BlockSpec(memory_space=pltpu.HBM)
    sem = pltpu.SemaphoreType.DMA
    coup_lanes = -(-subs * inner_rows // 128) * 128

    def vmem(kind, *dims):
        return pltpu.VMEM(tuple(max(d, 1) for d in dims), kind)

    return pl.pallas_call(
        functools.partial(kernel, n_sub, n_blk, pad, main, extra),
        out_shape=jax.ShapeDtypeStruct((subs, inner_rows, cols), BF16),
        in_specs=[hbm] * 7,
        out_specs=pl.BlockSpec(memory_space=pltpu.VMEM),
        scratch_shapes=[
            vmem(BF16, subs, order, quarter),
            vmem(BF16, n_blk, subs, quarter, cols),
            vmem(F32, subs, order, cols),
            vmem(BF16, tile, slots, cols),
            vmem(BF16, mine, 2, slots, cols),
            vmem(BF16, mine, slots, cols),
            vmem(BF16, mine, slots, cols),
            vmem(BF16, mine, slots, cols),
            vmem(BF16, n_sub * pad, cols),
            vmem(BF16, n_sub * pad, cols),
            vmem(BF16, mine, n_sub * main, cols),
            vmem(BF16, mine, n_sub * main, cols),
            vmem(BF16, n_sub * extra, cols),
            vmem(BF16, n_sub * extra, cols),
            vmem(F32, order, coup_lanes),
            vmem(BF16, tile, subs * inner_rows, slots_one),
            vmem(BF16, n_blk, mine, subs * inner_rows, slots_one),
            vmem(F32, n_blk, subs, inner_rows, cols),
            vmem(F32, n_blk, subs, inner_rows, cols),
            vmem(BF16, slots, cols),
            vmem(BF16, subs, tile, slots_one),
            vmem(BF16, *coupling.shape),
            vmem(jnp.int32, *peer_device.shape),
            vmem(jnp.int32, *peer_lane.shape),
            pltpu.SMEM(blocks.shape, jnp.int32),
            sem((subs + 1,)),
            sem((5,)),
            sem((subs, 2)),
            sem((subs, 2)),
            sem((subs, 2)),
            sem((subs, mine, 2, 2)),
            sem((subs, mine, 2)),
            sem((2,)),
            sem((mine, 2)),
            sem((2,)),
            sem((3, 2)),
            sem((3, 2)),
        ],
        compiler_params=pltpu.CompilerParams(
            collective_id=0, has_side_effects=True, vmem_limit_bytes=56 * 1024 * 1024
        ),
        cost_estimate=pl.CostEstimate(
            flops=flops, bytes_accessed=2 * factor.size, transcendentals=0
        ),
    )(factor, samples, jnp.swapaxes(diagonal, 1, 2), coupling, blocks, peer_device, peer_lane)


def solution(mesh):
    placed = (
        P("sub", None, "blk"),
        P("sub", "blk", None),
        P("sub", None, None),
        P("sub", "blk", None),
        P("sub"),
        P("sub", None),
        P("sub", None),
        P("sub", None),
    )
    return jax.shard_map(
        local, mesh=mesh, in_specs=placed, out_specs=P("sub", "blk", None), check_vma=False
    )
```

```python
import functools

import jax
import jax.numpy as jnp
from jax import lax
from jax.experimental import pallas as pl
from jax.experimental.pallas import tpu as pltpu
from jax.sharding import PartitionSpec as P

FACE_HALF = 104
MESH = pl.DeviceIdType.MESH
F32, BF16 = jnp.float32, jnp.bfloat16


def kernel(
    n_sub, n_blk, pad, main, extra,
    factor, samples, diagonal, coupling, blocks_in, peer_in, lane_in_ref, out,
    fac, drv, tr, parts, near, far, mixed, kept, diag_out, diag_in, main_out, main_in,
    tail_out, tail_in, coup_t, coup_out, coup_in, inner, inner_in, diag_own,
    diag_raw, coup, peer_device, peer_lane, blocks,
    local_sem, small_sem, near_sem, far_sem, relay_sem, near_sum, far_sum, diag_sem, main_sem,
    tail_sem, coup_sem, last_sem,
):
    me, here = lax.axis_index("sub"), lax.axis_index("blk")
    subs, order, quarter = fac.shape
    tile, slots_one = diagonal.shape[1], diagonal.shape[2]
    slots = subs * slots_one
    cols = samples.shape[2]
    mine = tile // n_blk
    inner_rows = coupling.shape[1]
    twin = here + 1 - 2 * lax.rem(here, 2)
    cross = lax.rem(here + 2, n_blk)
    diag = lax.rem(twin + 2, n_blk)

    def remote(src, dst, sems, where):
        return pltpu.make_async_remote_copy(
            src_ref=src, dst_ref=dst, send_sem=sems.at[0], recv_sem=sems.at[1],
            device_id=where, device_id_type=MESH,
        )

    def sub_peer(step):
        return lax.rem(me + step, n_sub)

    def each_peer(act):
        if n_sub <= 2 * tile:
            for step in range(1, n_sub):
                act(step)
        else:
            lax.fori_loop(1, n_sub, lambda step, carry: act(step), None)

    barrier = pltpu.get_barrier_semaphore()
    for b in (twin, cross, diag):
        pl.semaphore_signal(barrier, inc=1, device_id={"blk": b}, device_id_type=MESH)

    def greet(step):
        pl.semaphore_signal(
            barrier, inc=1, device_id={"sub": sub_peer(step)}, device_id_type=MESH
        )

    each_peer(greet)

    small = [
        pltpu.make_async_copy(src, dst, small_sem.at[i])
        for i, (src, dst) in enumerate((
            (blocks_in, blocks), (peer_in, peer_device), (lane_in_ref, peer_lane),
            (diagonal, diag_raw), (coupling, coup),
        ))
    ]
    for c in small:
        c.start()
    own = pltpu.make_async_copy(samples, drv.at[here], local_sem.at[subs])
    own.start()
    load = []
    for s in range(subs):
        one = pltpu.make_async_copy(factor.at[s], fac.at[s], local_sem.at[s])
        one.start()
        load.append(one)

    pl.semaphore_wait(barrier, n_sub - 1 + 3)

    to_far = [
        remote(samples.at[s], drv.at[here, s], far_sem.at[s], {"blk": cross}) for s in range(subs)
    ]
    to_near = [
        remote(samples.at[s], drv.at[here, s], near_sem.at[s], {"blk": twin}) for s in range(subs)
    ]
    for s in range(subs):
        to_far[s].start()
    for s in range(subs):
        to_near[s].start()

    for c in small:
        c.wait()
    slot_of = lax.broadcasted_iota(jnp.int32, (1, slots_one), 1)
    peer_rows, peer_cols, lane_cols = [], [], []
    for s in range(subs):
        peer = jnp.where(slot_of < blocks[s], peer_device[pl.ds(s, 1), :], -1)
        peer_rows.append(peer)
        square = (slots_one, slots_one)
        peer_cols.append(jnp.broadcast_to(peer.astype(F32), square).T[:, :1])
        lanes = peer_lane[pl.ds(s, 1), :].astype(F32)
        lane_cols.append(jnp.broadcast_to(lanes, square).T[:, :1])
    peer_row = jnp.concatenate(peer_rows, axis=1)
    lane_row = jnp.concatenate([peer_lane[pl.ds(s, 1), :] for s in range(subs)], axis=1)
    peer_col = jnp.concatenate(peer_cols, axis=0).astype(jnp.int32)
    lane_col = jnp.concatenate(lane_cols, axis=0).astype(jnp.int32)
    live = peer_col >= 0
    inside = peer_col == me

    def target(peer, lane, size, low, high, offset):
        chosen = (peer >= 0) & (lane >= low) & (lane < high)
        return jnp.where(chosen, peer * size + (lane - low) + offset, -1)

    def place(size, low, high, offset=0):
        row_of = lax.broadcasted_iota(jnp.int32, (n_sub * size, slots), 0)
        wanted = target(peer_row, lane_row, size, low, high, offset)
        return jnp.where(row_of == wanted, 1.0, 0.0).astype(BF16)

    def collect(size, low, high, offset=0):
        lane_of = lax.broadcasted_iota(jnp.int32, (slots, n_sub * size), 1)
        wanted = target(peer_col, lane_col, size, low, high, offset)
        return jnp.where(lane_of == wanted, 1.0, 0.0).astype(BF16)

    def rows_of(index, size):
        return pl.ds(pl.multiple_of(index * size, 16), size)

    def send_faces(value, sent, got, sems, size):
        sent[...] = value.astype(BF16)
        got[rows_of(me, size), :] = sent[rows_of(me, size), :]

        def go(step):
            remote(
                sent.at[rows_of(sub_peer(step), size)], got.at[rows_of(me, size)], sems,
                {"sub": sub_peer(step)},
            ).start()

        each_peer(go)

    def wait_faces(sent, got, sems, size):
        every = pl.ds(0, (n_sub - 1) * size)
        remote(sent.at[every], got.at[every], sems, {"sub": sub_peer(1)}).wait()

    def dot(left, right):
        return jnp.dot(left, right, preferred_element_type=F32)

    for s in range(subs):
        wide = jnp.concatenate(
            [diag_raw[s].astype(F32), jnp.zeros((cols - tile, slots_one), F32)], axis=0
        )
        diag_own[s * slots_one:(s + 1) * slots_one, :] = wide.T.astype(BF16)
    send_faces(dot(place(pad, 0, pad), diag_own[...]), diag_out, diag_in, diag_sem, pad)

    own.wait()
    row_in = lax.broadcasted_iota(jnp.int32, (quarter, 1), 0)
    lane_in = lax.broadcasted_iota(jnp.int32, (1, quarter), 1)

    def first(s, b):
        begin = pl.multiple_of(b * quarter, quarter)
        rows_live = row_in + begin < blocks[s] * tile
        value = drv[b, s]
        value = jnp.where(rows_live, value, jnp.zeros_like(value))
        return lax.dot_general(
            value, fac[s, pl.ds(begin, quarter), :], (((0,), (0,)), ((), ())),
            preferred_element_type=F32,
        )

    near_copies, far_copies = {}, {}

    def spans(s):
        step = 1 if s == subs - 1 else mine
        return [(k, step) for k in range(0, mine, step)]

    def send_near(s):
        span = pl.ds(s * slots_one, slots_one)
        for j, group in ((1, diag), (0, twin)):
            for k, step in spans(s):
                c = remote(
                    parts.at[pl.ds(group * mine + k, step), span],
                    near.at[j, pl.ds(k, step), span], near_sum.at[s, k, j], {"blk": twin},
                )
                c.start()
                near_copies[s, k, j] = c

    def send_far(s):
        span = pl.ds(s * slots_one, slots_one)
        for k, step in spans(s):
            near_copies[s, k, 1].wait()
            mixed[k:k + step, span, :] = (
                parts[pl.ds(cross * mine + k, step), span, :].astype(F32)
                + near[1, k:k + step, span, :].astype(F32)
            ).astype(BF16)
            c = remote(
                mixed.at[k:k + step, span], far.at[k:k + step, span], far_sum.at[s, k],
                {"blk": cross},
            )
            c.start()
            far_copies[s, k] = c

    for s in range(subs):
        load[s].wait()
        reduced = first(s, here)
        to_near[s].wait()
        reduced += first(s, twin)
        to_far[s].wait()
        relay = remote(drv.at[cross, s], drv.at[cross, s], relay_sem.at[s], {"blk": twin})
        relay.start()
        reduced += first(s, cross)
        if s:
            send_far(s - 1)
        relay.wait()
        reduced += first(s, diag)
        alive = lane_in + here * quarter < blocks[s] * tile
        reduced = jnp.where(alive, reduced, 0.0).astype(BF16)
        for q in range(0, order, quarter):
            tr[s, q:q + quarter, :] = lax.dot_general(
                fac[s, q:q + quarter, :], reduced, (((1,), (1,)), ((), ())),
                preferred_element_type=F32,
            )
        for t in range(tile):
            parts[t, s * slots_one:(s + 1) * slots_one, :] = tr[
                s, pl.ds(t, slots_one, stride=tile), :
            ].astype(BF16)
        send_near(s)
    send_far(subs - 1)

    tail = None
    for k in range(mine):
        for s in range(subs):
            if (s, k) in far_copies:
                near_copies[s, k, 0].wait()
                far_copies[s, k].wait()
        kept[k] = (
            parts[here * mine + k].astype(F32) + near[0, k].astype(F32) + far[k].astype(F32)
        ).astype(BF16)
        if main:
            send_faces(
                dot(place(main, 0, main), kept[k]), main_out.at[k], main_in.at[k], main_sem.at[k],
                main,
            )
        if extra:
            got = dot(place(extra, main, pad, k * (extra // mine)), kept[k])
            tail = got if k == 0 else tail + got
    if extra:
        send_faces(tail, tail_out, tail_in, tail_sem, extra)

    wide = coup[...].reshape(subs * inner_rows, order).astype(F32)
    filler = jnp.zeros((coup_t.shape[1] - subs * inner_rows, order), F32)
    coup_t[...] = jnp.concatenate([wide, filler], axis=0).T
    for t in range(tile):
        piece = coup_t[pl.ds(t, slots_one, stride=tile), :].T
        coup_out[t] = piece[:subs * inner_rows].astype(BF16)
    coup_in[here] = coup_out[pl.ds(here * mine, mine)]
    coup_copies = [
        remote(coup_out.at[pl.ds(b * mine, mine)], coup_in.at[here], coup_sem.at[i], {"blk": b})
        for i, b in enumerate((twin, cross, diag))
    ]
    for c in coup_copies:
        c.start()

    def own_side(value):
        return jnp.where(inside, 0.0, value.astype(F32))

    wait_faces(diag_out, diag_in, diag_sem, pad)
    divisors = own_side(diag_own[...]) + dot(collect(pad, 0, pad), diag_in[...])
    lane_t = lax.broadcasted_iota(jnp.int32, (slots, cols), 1)
    divisor = []
    for k in range(mine):
        one = jnp.sum(jnp.where(lane_t == here * mine + k, divisors, 0.0), axis=1, keepdims=True)
        divisor.append(jnp.where(live, one, 1.0))
    for c in coup_copies:
        c.wait()
    total = []
    for k in range(mine):
        both = own_side(kept[k])
        if main:
            wait_faces(main_out.at[k], main_in.at[k], main_sem.at[k], main)
            both += dot(collect(main, 0, main), main_in[k])
        total.append(both)
    if extra:
        wait_faces(tail_out, tail_in, tail_sem, extra)
        for k in range(mine):
            total[k] += dot(collect(extra, main, pad, k * (extra // mine)), tail_in[...])
    sums = [None] * subs
    for k in range(mine):
        coef = jnp.where(live, total[k] / divisor[k], 0.0).astype(BF16)
        for s in range(subs):
            left = coup_in[:, k, s * inner_rows:(s + 1) * inner_rows, :]
            got = dot(
                left.reshape(n_blk * inner_rows, slots_one),
                coef[s * slots_one:(s + 1) * slots_one],
            )
            sums[s] = got if k == 0 else sums[s] + got
    for s in range(subs):
        inner[:, s] = sums[s].reshape(n_blk, inner_rows, cols)
    last = [
        remote(inner.at[b], inner_in.at[here], last_sem.at[i], {"blk": b})
        for i, b in enumerate((twin, cross, diag))
    ]
    for c in last:
        c.start()
    result = inner[here]
    for c in last:
        c.wait()
    for b in (twin, cross, diag):
        result = result + inner_in[b]
    out[...] = result


def local(factor, samples, diagonal, coupling, blocks, peer_device, peer_lane, owns_face):
    n_sub, n_blk = lax.axis_size("sub"), lax.axis_size("blk")
    subs, order, quarter = factor.shape
    slots_one, tile = diagonal.shape[1], diagonal.shape[2]
    slots, cols = subs * slots_one, samples.shape[2]
    mine, inner_rows = tile // n_blk, coupling.shape[1]
    half_cycle = (n_sub - 1) // 2
    capacity = (FACE_HALF + half_cycle - 1) // half_cycle
    pad = -(-capacity // 16) * 16
    main = capacity // 16 * 16
    extra = -(-(capacity - main) * mine // 16) * 16
    flops = 4 * subs * order * quarter * cols
    hbm = pl.BlockSpec(memory_space=pltpu.HBM)
    sem = pltpu.SemaphoreType.DMA
    coup_lanes = -(-subs * inner_rows // 128) * 128

    def vmem(kind, *dims):
        return pltpu.VMEM(tuple(max(d, 1) for d in dims), kind)

    return pl.pallas_call(
        functools.partial(kernel, n_sub, n_blk, pad, main, extra),
        out_shape=jax.ShapeDtypeStruct((subs, inner_rows, cols), F32),
        in_specs=[hbm] * 7,
        out_specs=pl.BlockSpec(memory_space=pltpu.VMEM),
        scratch_shapes=[
            vmem(BF16, subs, order, quarter),
            vmem(BF16, n_blk, subs, quarter, cols),
            vmem(F32, subs, order, cols),
            vmem(BF16, tile, slots, cols),
            vmem(BF16, 2, mine, slots, cols),
            vmem(BF16, mine, slots, cols),
            vmem(BF16, mine, slots, cols),
            vmem(BF16, mine, slots, cols),
            vmem(BF16, n_sub * pad, cols),
            vmem(BF16, n_sub * pad, cols),
            vmem(BF16, mine, n_sub * main, cols),
            vmem(BF16, mine, n_sub * main, cols),
            vmem(BF16, n_sub * extra, cols),
            vmem(BF16, n_sub * extra, cols),
            vmem(F32, order, coup_lanes),
            vmem(BF16, tile, subs * inner_rows, slots_one),
            vmem(BF16, n_blk, mine, subs * inner_rows, slots_one),
            vmem(F32, n_blk, subs, inner_rows, cols),
            vmem(F32, n_blk, subs, inner_rows, cols),
            vmem(BF16, slots, cols),
            vmem(BF16, subs, tile, slots_one),
            vmem(BF16, *coupling.shape),
            vmem(jnp.int32, *peer_device.shape),
            vmem(jnp.int32, *peer_lane.shape),
            pltpu.SMEM(blocks.shape, jnp.int32),
            sem((subs + 1,)),
            sem((5,)),
            sem((subs, 2)),
            sem((subs, 2)),
            sem((subs, 2)),
            sem((subs, mine, 2, 2)),
            sem((subs, mine, 2)),
            sem((2,)),
            sem((mine, 2)),
            sem((2,)),
            sem((3, 2)),
            sem((3, 2)),
        ],
        compiler_params=pltpu.CompilerParams(
            collective_id=0, has_side_effects=True, vmem_limit_bytes=56 * 1024 * 1024
        ),
        cost_estimate=pl.CostEstimate(
            flops=flops, bytes_accessed=2 * factor.size, transcendentals=0
        ),
    )(factor, samples, jnp.swapaxes(diagonal, 1, 2), coupling, blocks, peer_device, peer_lane).astype(BF16)


def solution(mesh):
    placed = (
        P("sub", None, "blk"),
        P("sub", "blk", None),
        P("sub", None, None),
        P("sub", "blk", None),
        P("sub"),
        P("sub", None),
        P("sub", None),
        P("sub", None),
    )
    return jax.shard_map(
        local, mesh=mesh, in_specs=placed, out_specs=P("sub", "blk", None), check_vma=False
    )
```

```python
import functools

import jax
import jax.numpy as jnp
from jax import lax
from jax.experimental import pallas as pl
from jax.experimental.pallas import tpu as pltpu
from jax.sharding import PartitionSpec as P

FACE_HALF = 104
MESH = pl.DeviceIdType.MESH
F32, BF16 = jnp.float32, jnp.bfloat16


def kernel(
    n_sub, n_blk, pad, main, extra,
    factor, samples, diagonal, coupling, blocks_in, peer_in, lane_in_ref, out,
    fac, drv, tr, parts, near, far, mixed, kept, diag_out, diag_in, main_out, main_in,
    tail_out, tail_in, coup_t, coup_out, coup_in, inner, inner_in, diag_own,
    diag_raw, coup, peer_device, peer_lane, blocks,
    local_sem, small_sem, near_sem, far_sem, relay_sem, near_sum, far_sum, diag_sem, main_sem,
    tail_sem, coup_sem, last_sem,
):
    me, here = lax.axis_index("sub"), lax.axis_index("blk")
    subs, order, quarter = fac.shape
    tile, slots_one = diagonal.shape[1], diagonal.shape[2]
    slots = subs * slots_one
    cols = samples.shape[2]
    mine = tile // n_blk
    inner_rows = coupling.shape[1]
    twin = here + 1 - 2 * lax.rem(here, 2)
    cross = lax.rem(here + 2, n_blk)
    diag = lax.rem(twin + 2, n_blk)

    def remote(src, dst, sems, where):
        return pltpu.make_async_remote_copy(
            src_ref=src, dst_ref=dst, send_sem=sems.at[0], recv_sem=sems.at[1],
            device_id=where, device_id_type=MESH,
        )

    def sub_peer(step):
        return lax.rem(me + step, n_sub)

    def each_peer(act):
        if n_sub <= 2 * tile:
            for step in range(1, n_sub):
                act(step)
        else:
            lax.fori_loop(1, n_sub, lambda step, carry: act(step), None)

    barrier = pltpu.get_barrier_semaphore()
    for b in (twin, cross, diag):
        pl.semaphore_signal(barrier, inc=1, device_id={"blk": b}, device_id_type=MESH)

    def greet(step):
        pl.semaphore_signal(
            barrier, inc=1, device_id={"sub": sub_peer(step)}, device_id_type=MESH
        )

    each_peer(greet)

    small = [
        pltpu.make_async_copy(src, dst, small_sem.at[i])
        for i, (src, dst) in enumerate((
            (blocks_in, blocks), (peer_in, peer_device), (lane_in_ref, peer_lane),
            (diagonal, diag_raw), (coupling, coup),
        ))
    ]
    for c in small:
        c.start()
    own = pltpu.make_async_copy(samples, drv.at[here], local_sem.at[subs])
    own.start()
    load = []
    for s in range(subs):
        one = pltpu.make_async_copy(factor.at[s], fac.at[s], local_sem.at[s])
        one.start()
        load.append(one)

    pl.semaphore_wait(barrier, n_sub - 1 + 3)

    to_far = [
        remote(samples.at[s], drv.at[here, s], far_sem.at[s], {"blk": cross}) for s in range(subs)
    ]
    to_near = [
        remote(samples.at[s], drv.at[here, s], near_sem.at[s], {"blk": twin}) for s in range(subs)
    ]
    to_far[0].start()
    for s in range(subs):
        to_near[s].start()

    for c in small:
        c.wait()
    slot_of = lax.broadcasted_iota(jnp.int32, (1, slots_one), 1)
    peer_rows, peer_cols, lane_cols = [], [], []
    for s in range(subs):
        peer = jnp.where(slot_of < blocks[s], peer_device[pl.ds(s, 1), :], -1)
        peer_rows.append(peer)
        square = (slots_one, slots_one)
        peer_cols.append(jnp.broadcast_to(peer.astype(F32), square).T[:, :1])
        lanes = peer_lane[pl.ds(s, 1), :].astype(F32)
        lane_cols.append(jnp.broadcast_to(lanes, square).T[:, :1])
    peer_row = jnp.concatenate(peer_rows, axis=1)
    lane_row = jnp.concatenate([peer_lane[pl.ds(s, 1), :] for s in range(subs)], axis=1)
    peer_col = jnp.concatenate(peer_cols, axis=0).astype(jnp.int32)
    lane_col = jnp.concatenate(lane_cols, axis=0).astype(jnp.int32)
    live = peer_col >= 0
    inside = peer_col == me

    def target(peer, lane, size, low, high, offset):
        chosen = (peer >= 0) & (lane >= low) & (lane < high)
        return jnp.where(chosen, peer * size + (lane - low) + offset, -1)

    def place(size, low, high, offset=0):
        row_of = lax.broadcasted_iota(jnp.int32, (n_sub * size, slots), 0)
        wanted = target(peer_row, lane_row, size, low, high, offset)
        return jnp.where(row_of == wanted, 1.0, 0.0).astype(BF16)

    def collect(size, low, high, offset=0):
        lane_of = lax.broadcasted_iota(jnp.int32, (slots, n_sub * size), 1)
        wanted = target(peer_col, lane_col, size, low, high, offset)
        return jnp.where(lane_of == wanted, 1.0, 0.0).astype(BF16)

    def rows_of(index, size):
        return pl.ds(pl.multiple_of(index * size, 16), size)

    def send_faces(value, sent, got, sems, size):
        sent[...] = value.astype(BF16)
        got[rows_of(me, size), :] = sent[rows_of(me, size), :]

        def go(step):
            remote(
                sent.at[rows_of(sub_peer(step), size)], got.at[rows_of(me, size)], sems,
                {"sub": sub_peer(step)},
            ).start()

        each_peer(go)

    def wait_faces(sent, got, sems, size):
        every = pl.ds(0, (n_sub - 1) * size)
        remote(sent.at[every], got.at[every], sems, {"sub": sub_peer(1)}).wait()

    def dot(left, right):
        return jnp.dot(left, right, preferred_element_type=F32)

    for s in range(subs):
        wide = jnp.concatenate(
            [diag_raw[s].astype(F32), jnp.zeros((cols - tile, slots_one), F32)], axis=0
        )
        diag_own[s * slots_one:(s + 1) * slots_one, :] = wide.T.astype(BF16)
    send_faces(dot(place(pad, 0, pad), diag_own[...]), diag_out, diag_in, diag_sem, pad)

    own.wait()
    for s in range(1, subs):
        to_far[s - 1].wait_send()
        to_far[s].start()
    row_in = lax.broadcasted_iota(jnp.int32, (quarter, 1), 0)
    lane_in = lax.broadcasted_iota(jnp.int32, (1, quarter), 1)

    def first(s, b):
        begin = pl.multiple_of(b * quarter, quarter)
        rows_live = row_in + begin < blocks[s] * tile
        value = drv[b, s]
        value = jnp.where(rows_live, value, jnp.zeros_like(value))
        return lax.dot_general(
            value, fac[s, pl.ds(begin, quarter), :], (((0,), (0,)), ((), ())),
            preferred_element_type=F32,
        )

    near_copies, far_copies = {}, {}

    def spans(s):
        step = 1 if s == subs - 1 else mine
        return [(k, step) for k in range(0, mine, step)]

    def send_near(s):
        span = pl.ds(s * slots_one, slots_one)
        for j, group in ((1, diag), (0, twin)):
            for k, step in spans(s):
                c = remote(
                    parts.at[pl.ds(group * mine + k, step), span],
                    near.at[j, pl.ds(k, step), span], near_sum.at[s, k, j], {"blk": twin},
                )
                c.start()
                near_copies[s, k, j] = c

    def send_far(s, k, step):
        span = pl.ds(s * slots_one, slots_one)
        near_copies[s, k, 1].wait()
        mixed[k:k + step, span, :] = (
            parts[pl.ds(cross * mine + k, step), span, :].astype(F32)
            + near[1, k:k + step, span, :].astype(F32)
        ).astype(BF16)
        c = remote(
            mixed.at[k:k + step, span], far.at[k:k + step, span], far_sum.at[s, k],
            {"blk": cross},
        )
        c.start()
        far_copies[s, k] = c

    for s in range(subs):
        load[s].wait()
        reduced = first(s, here)
        to_near[s].wait()
        reduced += first(s, twin)
        if s == subs - 1:
            to_far[s].wait_send()
        to_far[s].wait_recv()
        relay = remote(drv.at[cross, s], drv.at[cross, s], relay_sem.at[s], {"blk": twin})
        relay.start()
        reduced += first(s, cross)
        if s > 1:
            far_copies[s - 2, 0].wait_send()
        if s:
            send_far(s - 1, 0, mine)
        relay.wait()
        reduced += first(s, diag)
        alive = lane_in + here * quarter < blocks[s] * tile
        reduced = jnp.where(alive, reduced, 0.0).astype(BF16)
        for q in range(0, order, quarter):
            tr[s, q:q + quarter, :] = lax.dot_general(
                fac[s, q:q + quarter, :], reduced, (((1,), (1,)), ((), ())),
                preferred_element_type=F32,
            )
        for t in range(tile):
            parts[t, s * slots_one:(s + 1) * slots_one, :] = tr[
                s, pl.ds(t, slots_one, stride=tile), :
            ].astype(BF16)
        send_near(s)
    if subs > 1:
        far_copies[subs - 2, 0].wait_send()
    send_far(subs - 1, 0, 1)

    tail = None
    for k in range(mine):
        far_copies[subs - 1, k].wait_send()
        if k + 1 < mine:
            send_far(subs - 1, k + 1, 1)
        for s in range(subs):
            if (s, k) in far_copies:
                near_copies[s, k, 0].wait()
                far_copies[s, k].wait_recv()
        kept[k] = (
            parts[here * mine + k].astype(F32) + near[0, k].astype(F32) + far[k].astype(F32)
        ).astype(BF16)
        if main:
            send_faces(
                dot(place(main, 0, main), kept[k]), main_out.at[k], main_in.at[k], main_sem.at[k],
                main,
            )
        if extra:
            got = dot(place(extra, main, pad, k * (extra // mine)), kept[k])
            tail = got if k == 0 else tail + got
    if extra:
        send_faces(tail, tail_out, tail_in, tail_sem, extra)

    wide = coup[...].reshape(subs * inner_rows, order).astype(F32)
    filler = jnp.zeros((coup_t.shape[1] - subs * inner_rows, order), F32)
    coup_t[...] = jnp.concatenate([wide, filler], axis=0).T
    for t in range(tile):
        piece = coup_t[pl.ds(t, slots_one, stride=tile), :].T
        coup_out[t] = piece[:subs * inner_rows].astype(BF16)
    coup_in[here] = coup_out[pl.ds(here * mine, mine)]
    coup_copies = [
        remote(coup_out.at[pl.ds(b * mine, mine)], coup_in.at[here], coup_sem.at[i], {"blk": b})
        for i, b in enumerate((twin, cross, diag))
    ]
    for c in coup_copies:
        c.start()

    def own_side(value):
        return jnp.where(inside, 0.0, value.astype(F32))

    wait_faces(diag_out, diag_in, diag_sem, pad)
    divisors = own_side(diag_own[...]) + dot(collect(pad, 0, pad), diag_in[...])
    lane_t = lax.broadcasted_iota(jnp.int32, (slots, cols), 1)
    divisor = []
    for k in range(mine):
        one = jnp.sum(jnp.where(lane_t == here * mine + k, divisors, 0.0), axis=1, keepdims=True)
        divisor.append(jnp.where(live, one, 1.0))
    for c in coup_copies:
        c.wait()
    total = []
    for k in range(mine):
        both = own_side(kept[k])
        if main:
            wait_faces(main_out.at[k], main_in.at[k], main_sem.at[k], main)
            both += dot(collect(main, 0, main), main_in[k])
        total.append(both)
    if extra:
        wait_faces(tail_out, tail_in, tail_sem, extra)
        for k in range(mine):
            total[k] += dot(collect(extra, main, pad, k * (extra // mine)), tail_in[...])
    sums = [None] * subs
    for k in range(mine):
        coef = jnp.where(live, total[k] / divisor[k], 0.0).astype(BF16)
        for s in range(subs):
            left = coup_in[:, k, s * inner_rows:(s + 1) * inner_rows, :]
            got = dot(
                left.reshape(n_blk * inner_rows, slots_one),
                coef[s * slots_one:(s + 1) * slots_one],
            )
            sums[s] = got if k == 0 else sums[s] + got
    for s in range(subs):
        inner[:, s] = sums[s].reshape(n_blk, inner_rows, cols)
    last = [
        remote(inner.at[b], inner_in.at[here], last_sem.at[i], {"blk": b})
        for i, b in enumerate((twin, cross, diag))
    ]
    for c in last:
        c.start()
    result = inner[here]
    for c in last:
        c.wait()
    for b in (twin, cross, diag):
        result = result + inner_in[b]
    out[...] = result


def local(factor, samples, diagonal, coupling, blocks, peer_device, peer_lane, owns_face):
    n_sub, n_blk = lax.axis_size("sub"), lax.axis_size("blk")
    subs, order, quarter = factor.shape
    slots_one, tile = diagonal.shape[1], diagonal.shape[2]
    slots, cols = subs * slots_one, samples.shape[2]
    mine, inner_rows = tile // n_blk, coupling.shape[1]
    half_cycle = (n_sub - 1) // 2
    capacity = (FACE_HALF + half_cycle - 1) // half_cycle
    pad = -(-capacity // 16) * 16
    main = capacity // 16 * 16
    extra = -(-(capacity - main) * mine // 16) * 16
    flops = 4 * subs * order * quarter * cols
    hbm = pl.BlockSpec(memory_space=pltpu.HBM)
    sem = pltpu.SemaphoreType.DMA
    coup_lanes = -(-subs * inner_rows // 128) * 128

    def vmem(kind, *dims):
        return pltpu.VMEM(tuple(max(d, 1) for d in dims), kind)

    return pl.pallas_call(
        functools.partial(kernel, n_sub, n_blk, pad, main, extra),
        out_shape=jax.ShapeDtypeStruct((subs, inner_rows, cols), F32),
        in_specs=[hbm] * 7,
        out_specs=pl.BlockSpec(memory_space=pltpu.VMEM),
        scratch_shapes=[
            vmem(BF16, subs, order, quarter),
            vmem(BF16, n_blk, subs, quarter, cols),
            vmem(F32, subs, order, cols),
            vmem(BF16, tile, slots, cols),
            vmem(BF16, 2, mine, slots, cols),
            vmem(BF16, mine, slots, cols),
            vmem(BF16, mine, slots, cols),
            vmem(BF16, mine, slots, cols),
            vmem(BF16, n_sub * pad, cols),
            vmem(BF16, n_sub * pad, cols),
            vmem(BF16, mine, n_sub * main, cols),
            vmem(BF16, mine, n_sub * main, cols),
            vmem(BF16, n_sub * extra, cols),
            vmem(BF16, n_sub * extra, cols),
            vmem(F32, order, coup_lanes),
            vmem(BF16, tile, subs * inner_rows, slots_one),
            vmem(BF16, n_blk, mine, subs * inner_rows, slots_one),
            vmem(F32, n_blk, subs, inner_rows, cols),
            vmem(F32, n_blk, subs, inner_rows, cols),
            vmem(BF16, slots, cols),
            vmem(BF16, subs, tile, slots_one),
            vmem(BF16, *coupling.shape),
            vmem(jnp.int32, *peer_device.shape),
            vmem(jnp.int32, *peer_lane.shape),
            pltpu.SMEM(blocks.shape, jnp.int32),
            sem((subs + 1,)),
            sem((5,)),
            sem((subs, 2)),
            sem((subs, 2)),
            sem((subs, 2)),
            sem((subs, mine, 2, 2)),
            sem((subs, mine, 2)),
            sem((2,)),
            sem((mine, 2)),
            sem((2,)),
            sem((3, 2)),
            sem((3, 2)),
        ],
        compiler_params=pltpu.CompilerParams(
            collective_id=0, has_side_effects=True, vmem_limit_bytes=56 * 1024 * 1024
        ),
        cost_estimate=pl.CostEstimate(
            flops=flops, bytes_accessed=2 * factor.size, transcendentals=0
        ),
    )(factor, samples, jnp.swapaxes(diagonal, 1, 2), coupling, blocks, peer_device, peer_lane).astype(BF16)


def solution(mesh):
    placed = (
        P("sub", None, "blk"),
        P("sub", "blk", None),
        P("sub", None, None),
        P("sub", "blk", None),
        P("sub"),
        P("sub", None),
        P("sub", None),
        P("sub", None),
    )
    return jax.shard_map(
        local, mesh=mesh, in_specs=placed, out_specs=P("sub", "blk", None), check_vma=False
    )
```

```python
import functools

import jax
import jax.numpy as jnp
from jax import lax
from jax.experimental import pallas as pl
from jax.experimental.pallas import tpu as pltpu
from jax.sharding import PartitionSpec as P

FACE_HALF = 104
MESH = pl.DeviceIdType.MESH
F32, BF16 = jnp.float32, jnp.bfloat16


def kernel(
    n_sub, n_blk, pad, main, extra,
    factor, samples, diagonal, coupling, blocks_in, peer_in, lane_in_ref, out,
    fac, drv, tr, parts, near, far, mixed, kept, diag_out, diag_in, main_out, main_in,
    tail_out, tail_in, coup_t, coup_out, coup_in, inner, inner_in, diag_own,
    diag_raw, coup, peer_device, peer_lane, blocks,
    local_sem, small_sem, near_sem, far_sem, relay_sem, near_sum, far_sum, diag_sem, main_sem,
    tail_sem, coup_sem, last_sem,
):
    me, here = lax.axis_index("sub"), lax.axis_index("blk")
    subs, order, quarter = fac.shape
    tile, slots_one = diagonal.shape[1], diagonal.shape[2]
    slots = subs * slots_one
    cols = samples.shape[2]
    mine = tile // n_blk
    inner_rows = coupling.shape[1]
    twin = here + 1 - 2 * lax.rem(here, 2)
    cross = lax.rem(here + 2, n_blk)
    diag = lax.rem(twin + 2, n_blk)

    def remote(src, dst, sems, where):
        return pltpu.make_async_remote_copy(
            src_ref=src, dst_ref=dst, send_sem=sems.at[0], recv_sem=sems.at[1],
            device_id=where, device_id_type=MESH,
        )

    def sub_peer(step):
        return lax.rem(me + step, n_sub)

    def each_peer(act):
        if n_sub <= 2 * tile:
            for step in range(1, n_sub):
                act(step)
        else:
            lax.fori_loop(1, n_sub, lambda step, carry: act(step), None)

    barrier = pltpu.get_barrier_semaphore()
    for b in (twin, cross, diag):
        pl.semaphore_signal(barrier, inc=1, device_id={"blk": b}, device_id_type=MESH)

    def greet(step):
        pl.semaphore_signal(
            barrier, inc=1, device_id={"sub": sub_peer(step)}, device_id_type=MESH
        )

    each_peer(greet)

    small = [
        pltpu.make_async_copy(src, dst, small_sem.at[i])
        for i, (src, dst) in enumerate((
            (blocks_in, blocks), (peer_in, peer_device), (lane_in_ref, peer_lane),
            (diagonal, diag_raw), (coupling, coup),
        ))
    ]
    for c in small:
        c.start()
    own = pltpu.make_async_copy(samples, drv.at[here], local_sem.at[subs])
    own.start()
    load = []
    for s in range(subs):
        one = pltpu.make_async_copy(factor.at[s], fac.at[s], local_sem.at[s])
        one.start()
        load.append(one)

    pl.semaphore_wait(barrier, n_sub - 1 + 3)

    to_far = [
        remote(samples.at[s], drv.at[here, s], far_sem.at[s], {"blk": cross}) for s in range(subs)
    ]
    to_near = [
        remote(samples.at[s], drv.at[here, s], near_sem.at[s], {"blk": twin}) for s in range(subs)
    ]
    for s in range(subs):
        to_far[s].start()
    for s in range(subs):
        to_near[s].start()

    for c in small:
        c.wait()
    slot_of = lax.broadcasted_iota(jnp.int32, (1, slots_one), 1)
    peer_rows, peer_cols, lane_cols = [], [], []
    for s in range(subs):
        peer = jnp.where(slot_of < blocks[s], peer_device[pl.ds(s, 1), :], -1)
        peer_rows.append(peer)
        square = (slots_one, slots_one)
        peer_cols.append(jnp.broadcast_to(peer.astype(F32), square).T[:, :1])
        lanes = peer_lane[pl.ds(s, 1), :].astype(F32)
        lane_cols.append(jnp.broadcast_to(lanes, square).T[:, :1])
    peer_row = jnp.concatenate(peer_rows, axis=1)
    lane_row = jnp.concatenate([peer_lane[pl.ds(s, 1), :] for s in range(subs)], axis=1)
    peer_col = jnp.concatenate(peer_cols, axis=0).astype(jnp.int32)
    lane_col = jnp.concatenate(lane_cols, axis=0).astype(jnp.int32)
    live = peer_col >= 0
    inside = peer_col == me

    def target(peer, lane, size, low, high, offset):
        chosen = (peer >= 0) & (lane >= low) & (lane < high)
        return jnp.where(chosen, peer * size + (lane - low) + offset, -1)

    def place(size, low, high, offset=0):
        row_of = lax.broadcasted_iota(jnp.int32, (n_sub * size, slots), 0)
        wanted = target(peer_row, lane_row, size, low, high, offset)
        return jnp.where(row_of == wanted, 1.0, 0.0).astype(BF16)

    def collect(size, low, high, offset=0):
        lane_of = lax.broadcasted_iota(jnp.int32, (slots, n_sub * size), 1)
        wanted = target(peer_col, lane_col, size, low, high, offset)
        return jnp.where(lane_of == wanted, 1.0, 0.0).astype(BF16)

    def rows_of(index, size):
        return pl.ds(pl.multiple_of(index * size, 16), size)

    def send_faces(value, sent, got, sems, size):
        sent[...] = value.astype(BF16)
        got[rows_of(me, size), :] = sent[rows_of(me, size), :]

        def go(step):
            remote(
                sent.at[rows_of(sub_peer(step), size)], got.at[rows_of(me, size)], sems,
                {"sub": sub_peer(step)},
            ).start()

        each_peer(go)

    def wait_faces(sent, got, sems, size):
        every = pl.ds(0, (n_sub - 1) * size)
        remote(sent.at[every], got.at[every], sems, {"sub": sub_peer(1)}).wait()

    def dot(left, right):
        return jnp.dot(left, right, preferred_element_type=F32)

    for s in range(subs):
        wide = jnp.concatenate(
            [diag_raw[s].astype(F32), jnp.zeros((cols - tile, slots_one), F32)], axis=0
        )
        diag_own[s * slots_one:(s + 1) * slots_one, :] = wide.T.astype(BF16)
    send_faces(dot(place(pad, 0, pad), diag_own[...]), diag_out, diag_in, diag_sem, pad)

    own.wait()
    row_in = lax.broadcasted_iota(jnp.int32, (quarter, 1), 0)
    lane_in = lax.broadcasted_iota(jnp.int32, (1, quarter), 1)

    def first(s, b):
        begin = pl.multiple_of(b * quarter, quarter)
        rows_live = row_in + begin < blocks[s] * tile
        value = drv[b, s]
        value = jnp.where(rows_live, value, jnp.zeros_like(value))
        return lax.dot_general(
            value, fac[s, pl.ds(begin, quarter), :], (((0,), (0,)), ((), ())),
            preferred_element_type=F32,
        )

    near_copies, far_copies = {}, {}

    def spans(s):
        step = 1 if s == subs - 1 else mine
        return [(k, step) for k in range(0, mine, step)]

    def send_near(s, j, k, step):
        span = pl.ds(s * slots_one, slots_one)
        group = diag if j else twin
        c = remote(
            parts.at[pl.ds(group * mine + k, step), span],
            near.at[j, pl.ds(k, step), span], near_sum.at[s, k, j], {"blk": twin},
        )
        c.start()
        near_copies[s, k, j] = c

    def send_far(s):
        span = pl.ds(s * slots_one, slots_one)
        for k, step in spans(s):
            near_copies[s, k, 1].wait()
            mixed[k:k + step, span, :] = (
                parts[pl.ds(cross * mine + k, step), span, :].astype(F32)
                + near[1, k:k + step, span, :].astype(F32)
            ).astype(BF16)
            c = remote(
                mixed.at[k:k + step, span], far.at[k:k + step, span], far_sum.at[s, k],
                {"blk": cross},
            )
            c.start()
            far_copies[s, k] = c

    for s in range(subs):
        load[s].wait()
        reduced = first(s, here)
        to_near[s].wait()
        reduced += first(s, twin)
        to_far[s].wait()
        relay = remote(drv.at[cross, s], drv.at[cross, s], relay_sem.at[s], {"blk": twin})
        relay.start()
        reduced += first(s, cross)
        if s:
            send_far(s - 1)
        relay.wait()
        reduced += first(s, diag)
        alive = lane_in + here * quarter < blocks[s] * tile
        reduced = jnp.where(alive, reduced, 0.0).astype(BF16)
        for q in range(0, order, quarter):
            tr[s, q:q + quarter, :] = lax.dot_general(
                fac[s, q:q + quarter, :], reduced, (((1,), (1,)), ((), ())),
                preferred_element_type=F32,
            )
        for k, step in spans(s):
            for t in range(tile):
                if k <= t % mine < k + step:
                    parts[t, s * slots_one:(s + 1) * slots_one, :] = tr[
                        s, pl.ds(t, slots_one, stride=tile), :
                    ].astype(BF16)
            send_near(s, 1, k, step)
        for k, step in spans(s):
            send_near(s, 0, k, step)
    send_far(subs - 1)

    tail, both_size = None, main + extra
    for k in range(mine):
        for s in range(subs):
            if (s, k) in far_copies:
                near_copies[s, k, 0].wait()
                far_copies[s, k].wait()
        kept[k] = (
            parts[here * mine + k].astype(F32) + near[0, k].astype(F32) + far[k].astype(F32)
        ).astype(BF16)
        if main and k + 1 < mine:
            send_faces(
                dot(place(main, 0, main), kept[k]), main_out.at[k], main_in.at[k], main_sem.at[k],
                main,
            )
        got = dot(place(both_size, main, pad, main + k * (extra // mine)), kept[k])
        tail = got if k == 0 else tail + got
    tail += dot(place(both_size, 0, main), kept[mine - 1])
    send_faces(tail, tail_out, tail_in, tail_sem, both_size)

    wide = coup[...].reshape(subs * inner_rows, order).astype(F32)
    filler = jnp.zeros((coup_t.shape[1] - subs * inner_rows, order), F32)
    coup_t[...] = jnp.concatenate([wide, filler], axis=0).T
    for t in range(tile):
        piece = coup_t[pl.ds(t, slots_one, stride=tile), :].T
        coup_out[t] = piece[:subs * inner_rows].astype(BF16)
    coup_in[here] = coup_out[pl.ds(here * mine, mine)]
    coup_copies = [
        remote(coup_out.at[pl.ds(b * mine, mine)], coup_in.at[here], coup_sem.at[i], {"blk": b})
        for i, b in enumerate((twin, cross, diag))
    ]
    for c in coup_copies:
        c.start()

    def own_side(value):
        return jnp.where(inside, 0.0, value.astype(F32))

    wait_faces(diag_out, diag_in, diag_sem, pad)
    divisors = own_side(diag_own[...]) + dot(collect(pad, 0, pad), diag_in[...])
    lane_t = lax.broadcasted_iota(jnp.int32, (slots, cols), 1)
    divisor = []
    for k in range(mine):
        one = jnp.sum(jnp.where(lane_t == here * mine + k, divisors, 0.0), axis=1, keepdims=True)
        divisor.append(jnp.where(live, one, 1.0))
    for c in coup_copies:
        c.wait()
    total = []
    for k in range(mine):
        both = own_side(kept[k])
        if main and k + 1 < mine:
            wait_faces(main_out.at[k], main_in.at[k], main_sem.at[k], main)
            both += dot(collect(main, 0, main), main_in[k])
        total.append(both)
    wait_faces(tail_out, tail_in, tail_sem, both_size)
    total[-1] += dot(collect(both_size, 0, main), tail_in[...])
    for k in range(mine):
        total[k] += dot(collect(both_size, main, pad, main + k * (extra // mine)), tail_in[...])
    sums = [None] * subs
    for k in range(mine):
        coef = jnp.where(live, total[k] / divisor[k], 0.0).astype(BF16)
        for s in range(subs):
            left = coup_in[:, k, s * inner_rows:(s + 1) * inner_rows, :]
            got = dot(
                left.reshape(n_blk * inner_rows, slots_one),
                coef[s * slots_one:(s + 1) * slots_one],
            )
            sums[s] = got if k == 0 else sums[s] + got
    for s in range(subs):
        inner[:, s] = sums[s].reshape(n_blk, inner_rows, cols)
    last = [
        remote(inner.at[b], inner_in.at[here], last_sem.at[i], {"blk": b})
        for i, b in enumerate((twin, cross, diag))
    ]
    for c in last:
        c.start()
    result = inner[here]
    for c in last:
        c.wait()
    for b in (twin, cross, diag):
        result = result + inner_in[b]
    out[...] = result


def local(factor, samples, diagonal, coupling, blocks, peer_device, peer_lane, owns_face):
    n_sub, n_blk = lax.axis_size("sub"), lax.axis_size("blk")
    subs, order, quarter = factor.shape
    slots_one, tile = diagonal.shape[1], diagonal.shape[2]
    slots, cols = subs * slots_one, samples.shape[2]
    mine, inner_rows = tile // n_blk, coupling.shape[1]
    half_cycle = (n_sub - 1) // 2
    capacity = (FACE_HALF + half_cycle - 1) // half_cycle
    pad = -(-capacity // 16) * 16
    main = capacity // 16 * 16
    extra = -(-(capacity - main) * mine // 16) * 16
    flops = 4 * subs * order * quarter * cols
    hbm = pl.BlockSpec(memory_space=pltpu.HBM)
    sem = pltpu.SemaphoreType.DMA
    coup_lanes = -(-subs * inner_rows // 128) * 128

    def vmem(kind, *dims):
        return pltpu.VMEM(tuple(max(d, 1) for d in dims), kind)

    return pl.pallas_call(
        functools.partial(kernel, n_sub, n_blk, pad, main, extra),
        out_shape=jax.ShapeDtypeStruct((subs, inner_rows, cols), F32),
        in_specs=[hbm] * 7,
        out_specs=pl.BlockSpec(memory_space=pltpu.VMEM),
        scratch_shapes=[
            vmem(BF16, subs, order, quarter),
            vmem(BF16, n_blk, subs, quarter, cols),
            vmem(F32, subs, order, cols),
            vmem(BF16, tile, slots, cols),
            vmem(BF16, 2, mine, slots, cols),
            vmem(BF16, mine, slots, cols),
            vmem(BF16, mine, slots, cols),
            vmem(BF16, mine, slots, cols),
            vmem(BF16, n_sub * pad, cols),
            vmem(BF16, n_sub * pad, cols),
            vmem(BF16, mine, n_sub * main, cols),
            vmem(BF16, mine, n_sub * main, cols),
            vmem(BF16, n_sub * (main + extra), cols),
            vmem(BF16, n_sub * (main + extra), cols),
            vmem(F32, order, coup_lanes),
            vmem(BF16, tile, subs * inner_rows, slots_one),
            vmem(BF16, n_blk, mine, subs * inner_rows, slots_one),
            vmem(F32, n_blk, subs, inner_rows, cols),
            vmem(F32, n_blk, subs, inner_rows, cols),
            vmem(BF16, slots, cols),
            vmem(BF16, subs, tile, slots_one),
            vmem(BF16, *coupling.shape),
            vmem(jnp.int32, *peer_device.shape),
            vmem(jnp.int32, *peer_lane.shape),
            pltpu.SMEM(blocks.shape, jnp.int32),
            sem((subs + 1,)),
            sem((5,)),
            sem((subs, 2)),
            sem((subs, 2)),
            sem((subs, 2)),
            sem((subs, mine, 2, 2)),
            sem((subs, mine, 2)),
            sem((2,)),
            sem((mine, 2)),
            sem((2,)),
            sem((3, 2)),
            sem((3, 2)),
        ],
        compiler_params=pltpu.CompilerParams(
            collective_id=0, has_side_effects=True, vmem_limit_bytes=56 * 1024 * 1024
        ),
        cost_estimate=pl.CostEstimate(
            flops=flops, bytes_accessed=2 * factor.size, transcendentals=0
        ),
    )(factor, samples, jnp.swapaxes(diagonal, 1, 2), coupling, blocks, peer_device, peer_lane).astype(BF16)


def solution(mesh):
    placed = (
        P("sub", None, "blk"),
        P("sub", "blk", None),
        P("sub", None, None),
        P("sub", "blk", None),
        P("sub"),
        P("sub", None),
        P("sub", None),
        P("sub", None),
    )
    return jax.shard_map(
        local, mesh=mesh, in_specs=placed, out_specs=P("sub", "blk", None), check_vma=False
    )
```

```python
import functools

import jax
import jax.numpy as jnp
from jax import lax
from jax.experimental import pallas as pl
from jax.experimental.pallas import tpu as pltpu
from jax.sharding import PartitionSpec as P

FACE_HALF = 104
MESH = pl.DeviceIdType.MESH
F32, BF16 = jnp.float32, jnp.bfloat16


def kernel(
    n_sub, n_blk, pad, main, extra,
    factor, samples, diagonal, coupling, blocks_in, peer_in, lane_in_ref, out,
    fac, drv, tr, parts, near, far, mixed, kept, diag_out, diag_in, main_out, main_in,
    tail_out, tail_in, coup_t, coup_out, coup_in, inner, inner_in, diag_own,
    diag_raw, coup, peer_device, peer_lane, blocks,
    local_sem, small_sem, near_sem, far_sem, relay_sem, near_sum, far_sum, diag_sem, main_sem,
    tail_sem, coup_sem, last_sem,
):
    me, here = lax.axis_index("sub"), lax.axis_index("blk")
    subs, order, quarter = fac.shape
    tile, slots_one = diagonal.shape[1], diagonal.shape[2]
    slots = subs * slots_one
    cols = samples.shape[2]
    mine = tile // n_blk
    inner_rows = coupling.shape[1]
    twin = here + 1 - 2 * lax.rem(here, 2)
    cross = lax.rem(here + 2, n_blk)
    diag = lax.rem(twin + 2, n_blk)

    def remote(src, dst, sems, where):
        return pltpu.make_async_remote_copy(
            src_ref=src, dst_ref=dst, send_sem=sems.at[0], recv_sem=sems.at[1],
            device_id=where, device_id_type=MESH,
        )

    def sub_peer(step):
        return lax.rem(me + step, n_sub)

    def each_peer(act):
        if n_sub <= 2 * tile:
            for step in sorted(range(1, n_sub), key=lambda step: abs(2 * step - n_sub)):
                act(step)
        else:
            lax.fori_loop(1, n_sub, lambda step, carry: act(step), None)

    barrier = pltpu.get_barrier_semaphore()
    for b in (twin, cross, diag):
        pl.semaphore_signal(barrier, inc=1, device_id={"blk": b}, device_id_type=MESH)

    def greet(step):
        pl.semaphore_signal(
            barrier, inc=1, device_id={"sub": sub_peer(step)}, device_id_type=MESH
        )

    each_peer(greet)

    small = [
        pltpu.make_async_copy(src, dst, small_sem.at[i])
        for i, (src, dst) in enumerate((
            (blocks_in, blocks), (peer_in, peer_device), (lane_in_ref, peer_lane),
            (diagonal, diag_raw), (coupling, coup),
        ))
    ]
    for c in small:
        c.start()
    own = pltpu.make_async_copy(samples, drv.at[here], local_sem.at[subs])
    own.start()
    load = []
    for s in range(subs):
        one = pltpu.make_async_copy(factor.at[s], fac.at[s], local_sem.at[s])
        one.start()
        load.append(one)

    pl.semaphore_wait(barrier, n_sub - 1 + 3)

    halves = [pl.ds(h * (quarter // 2), quarter // 2) for h in range(2)]
    to_far = [
        [
            remote(
                samples.at[s, half], drv.at[here, s, half], far_sem.at[s, h], {"blk": cross}
            )
            for h, half in enumerate(halves)
        ]
        for s in range(subs)
    ]
    to_near = [
        remote(samples.at[s], drv.at[here, s], near_sem.at[s], {"blk": twin}) for s in range(subs)
    ]
    for s in range(subs):
        for c in to_far[s]:
            c.start()
    for s in range(subs):
        to_near[s].start()

    for c in small:
        c.wait()
    slot_of = lax.broadcasted_iota(jnp.int32, (1, slots_one), 1)
    peer_rows, peer_cols, lane_cols = [], [], []
    for s in range(subs):
        peer = jnp.where(slot_of < blocks[s], peer_device[pl.ds(s, 1), :], -1)
        peer_rows.append(peer)
        square = (slots_one, slots_one)
        peer_cols.append(jnp.broadcast_to(peer.astype(F32), square).T[:, :1])
        lanes = peer_lane[pl.ds(s, 1), :].astype(F32)
        lane_cols.append(jnp.broadcast_to(lanes, square).T[:, :1])
    peer_row = jnp.concatenate(peer_rows, axis=1)
    lane_row = jnp.concatenate([peer_lane[pl.ds(s, 1), :] for s in range(subs)], axis=1)
    peer_col = jnp.concatenate(peer_cols, axis=0).astype(jnp.int32)
    lane_col = jnp.concatenate(lane_cols, axis=0).astype(jnp.int32)
    live = peer_col >= 0
    inside = peer_col == me

    def target(peer, lane, size, low, high, offset):
        chosen = (peer >= 0) & (lane >= low) & (lane < high)
        return jnp.where(chosen, peer * size + (lane - low) + offset, -1)

    def place(size, low, high, offset=0):
        row_of = lax.broadcasted_iota(jnp.int32, (n_sub * size, slots), 0)
        wanted = target(peer_row, lane_row, size, low, high, offset)
        return jnp.where(row_of == wanted, 1.0, 0.0).astype(BF16)

    def collect(size, low, high, offset=0):
        lane_of = lax.broadcasted_iota(jnp.int32, (slots, n_sub * size), 1)
        wanted = target(peer_col, lane_col, size, low, high, offset)
        return jnp.where(lane_of == wanted, 1.0, 0.0).astype(BF16)

    def rows_of(index, size):
        return pl.ds(pl.multiple_of(index * size, 16), size)

    def send_faces(value, sent, got, sems, size):
        sent[...] = value.astype(BF16)
        got[rows_of(me, size), :] = sent[rows_of(me, size), :]

        def go(step):
            remote(
                sent.at[rows_of(sub_peer(step), size)], got.at[rows_of(me, size)], sems,
                {"sub": sub_peer(step)},
            ).start()

        each_peer(go)

    def wait_faces(sent, got, sems, size):
        every = pl.ds(0, (n_sub - 1) * size)
        remote(sent.at[every], got.at[every], sems, {"sub": sub_peer(1)}).wait()

    def dot(left, right):
        return jnp.dot(left, right, preferred_element_type=F32)

    for s in range(subs):
        wide = jnp.concatenate(
            [diag_raw[s].astype(F32), jnp.zeros((cols - tile, slots_one), F32)], axis=0
        )
        diag_own[s * slots_one:(s + 1) * slots_one, :] = wide.T.astype(BF16)
    send_faces(dot(place(pad, 0, pad), diag_own[...]), diag_out, diag_in, diag_sem, pad)

    own.wait()
    row_in = lax.broadcasted_iota(jnp.int32, (quarter, 1), 0)
    lane_in = lax.broadcasted_iota(jnp.int32, (1, quarter), 1)

    def first(s, b):
        begin = pl.multiple_of(b * quarter, quarter)
        rows_live = row_in + begin < blocks[s] * tile
        value = drv[b, s]
        value = jnp.where(rows_live, value, jnp.zeros_like(value))
        return lax.dot_general(
            value, fac[s, pl.ds(begin, quarter), :], (((0,), (0,)), ((), ())),
            preferred_element_type=F32,
        )

    near_copies, far_copies = {}, {}

    def spans(s):
        step = 1 if s == subs - 1 else mine
        return [(k, step) for k in range(0, mine, step)]

    def send_near(s, j, k, step):
        span = pl.ds(s * slots_one, slots_one)
        group = diag if j else twin
        c = remote(
            parts.at[pl.ds(group * mine + k, step), span],
            near.at[j, pl.ds(k, step), span], near_sum.at[s, k, j], {"blk": twin},
        )
        c.start()
        near_copies[s, k, j] = c

    def send_far(s):
        span = pl.ds(s * slots_one, slots_one)
        for k, step in spans(s):
            near_copies[s, k, 1].wait()
            mixed[k:k + step, span, :] = (
                parts[pl.ds(cross * mine + k, step), span, :].astype(F32)
                + near[1, k:k + step, span, :].astype(F32)
            ).astype(BF16)
            c = remote(
                mixed.at[k:k + step, span], far.at[k:k + step, span], far_sum.at[s, k],
                {"blk": cross},
            )
            c.start()
            far_copies[s, k] = c

    for s in range(subs):
        load[s].wait()
        reduced = first(s, here)
        to_near[s].wait()
        reduced += first(s, twin)
        relays = []
        for h, half in enumerate(halves):
            to_far[s][h].wait()
            block = drv.at[cross, s, half]
            relay = remote(block, block, relay_sem.at[s, h], {"blk": twin})
            relay.start()
            relays.append(relay)
        reduced += first(s, cross)
        if s:
            send_far(s - 1)
        for relay in relays:
            relay.wait()
        reduced += first(s, diag)
        alive = lane_in + here * quarter < blocks[s] * tile
        reduced = jnp.where(alive, reduced, 0.0).astype(BF16)
        for q in range(0, order, quarter):
            tr[s, q:q + quarter, :] = lax.dot_general(
                fac[s, q:q + quarter, :], reduced, (((1,), (1,)), ((), ())),
                preferred_element_type=F32,
            )
        for k, step in spans(s):
            for t in range(tile):
                if k <= t % mine < k + step:
                    parts[t, s * slots_one:(s + 1) * slots_one, :] = tr[
                        s, pl.ds(t, slots_one, stride=tile), :
                    ].astype(BF16)
            send_near(s, 1, k, step)
        for k, step in spans(s):
            send_near(s, 0, k, step)
    send_far(subs - 1)

    tail, both_size = None, main + extra
    for k in range(mine):
        for s in range(subs):
            if (s, k) in far_copies:
                near_copies[s, k, 0].wait()
                far_copies[s, k].wait()
        kept[k] = (
            parts[here * mine + k].astype(F32) + near[0, k].astype(F32) + far[k].astype(F32)
        ).astype(BF16)
        if main and k + 1 < mine:
            send_faces(
                dot(place(main, 0, main), kept[k]), main_out.at[k], main_in.at[k], main_sem.at[k],
                main,
            )
        got = dot(place(both_size, main, pad, main + k * (extra // mine)), kept[k])
        tail = got if k == 0 else tail + got
    tail += dot(place(both_size, 0, main), kept[mine - 1])
    send_faces(tail, tail_out, tail_in, tail_sem, both_size)

    wide = coup[...].reshape(subs * inner_rows, order).astype(F32)
    filler = jnp.zeros((coup_t.shape[1] - subs * inner_rows, order), F32)
    coup_t[...] = jnp.concatenate([wide, filler], axis=0).T
    for t in range(tile):
        piece = coup_t[pl.ds(t, slots_one, stride=tile), :].T
        coup_out[t] = piece[:subs * inner_rows].astype(BF16)
    coup_in[here] = coup_out[pl.ds(here * mine, mine)]
    coup_copies = [
        remote(coup_out.at[pl.ds(b * mine, mine)], coup_in.at[here], coup_sem.at[i], {"blk": b})
        for i, b in enumerate((twin, cross, diag))
    ]
    for c in coup_copies:
        c.start()

    def own_side(value):
        return jnp.where(inside, 0.0, value.astype(F32))

    wait_faces(diag_out, diag_in, diag_sem, pad)
    divisors = own_side(diag_own[...]) + dot(collect(pad, 0, pad), diag_in[...])
    lane_t = lax.broadcasted_iota(jnp.int32, (slots, cols), 1)
    divisor = []
    for k in range(mine):
        one = jnp.sum(jnp.where(lane_t == here * mine + k, divisors, 0.0), axis=1, keepdims=True)
        divisor.append(jnp.where(live, one, 1.0))
    for c in coup_copies:
        c.wait()
    total = []
    for k in range(mine):
        both = own_side(kept[k])
        if main and k + 1 < mine:
            wait_faces(main_out.at[k], main_in.at[k], main_sem.at[k], main)
            both += dot(collect(main, 0, main), main_in[k])
        total.append(both)
    wait_faces(tail_out, tail_in, tail_sem, both_size)
    total[-1] += dot(collect(both_size, 0, main), tail_in[...])
    for k in range(mine):
        total[k] += dot(collect(both_size, main, pad, main + k * (extra // mine)), tail_in[...])
    sums = [None] * subs
    for k in range(mine):
        coef = jnp.where(live, total[k] / divisor[k], 0.0).astype(BF16)
        for s in range(subs):
            left = coup_in[:, k, s * inner_rows:(s + 1) * inner_rows, :]
            got = dot(
                left.reshape(n_blk * inner_rows, slots_one),
                coef[s * slots_one:(s + 1) * slots_one],
            )
            sums[s] = got if k == 0 else sums[s] + got
    for s in range(subs):
        inner[:, s] = sums[s].reshape(n_blk, inner_rows, cols)
    last = [
        remote(inner.at[b], inner_in.at[here], last_sem.at[i], {"blk": b})
        for i, b in enumerate((twin, cross, diag))
    ]
    for c in last:
        c.start()
    result = inner[here]
    for c in last:
        c.wait()
    for b in (twin, cross, diag):
        result = result + inner_in[b]
    out[...] = result


def local(factor, samples, diagonal, coupling, blocks, peer_device, peer_lane, owns_face):
    n_sub, n_blk = lax.axis_size("sub"), lax.axis_size("blk")
    subs, order, quarter = factor.shape
    slots_one, tile = diagonal.shape[1], diagonal.shape[2]
    slots, cols = subs * slots_one, samples.shape[2]
    mine, inner_rows = tile // n_blk, coupling.shape[1]
    half_cycle = (n_sub - 1) // 2
    capacity = (FACE_HALF + half_cycle - 1) // half_cycle
    pad = -(-capacity // 16) * 16
    main = capacity // 16 * 16
    extra = -(-(capacity - main) * mine // 16) * 16
    flops = 4 * subs * order * quarter * cols
    hbm = pl.BlockSpec(memory_space=pltpu.HBM)
    sem = pltpu.SemaphoreType.DMA
    coup_lanes = -(-subs * inner_rows // 128) * 128

    def vmem(kind, *dims):
        return pltpu.VMEM(tuple(max(d, 1) for d in dims), kind)

    return pl.pallas_call(
        functools.partial(kernel, n_sub, n_blk, pad, main, extra),
        out_shape=jax.ShapeDtypeStruct((subs, inner_rows, cols), F32),
        in_specs=[hbm] * 7,
        out_specs=pl.BlockSpec(memory_space=pltpu.VMEM),
        scratch_shapes=[
            vmem(BF16, subs, order, quarter),
            vmem(BF16, n_blk, subs, quarter, cols),
            vmem(F32, subs, order, cols),
            vmem(BF16, tile, slots, cols),
            vmem(BF16, 2, mine, slots, cols),
            vmem(BF16, mine, slots, cols),
            vmem(BF16, mine, slots, cols),
            vmem(BF16, mine, slots, cols),
            vmem(BF16, n_sub * pad, cols),
            vmem(BF16, n_sub * pad, cols),
            vmem(BF16, mine, n_sub * main, cols),
            vmem(BF16, mine, n_sub * main, cols),
            vmem(BF16, n_sub * (main + extra), cols),
            vmem(BF16, n_sub * (main + extra), cols),
            vmem(F32, order, coup_lanes),
            vmem(BF16, tile, subs * inner_rows, slots_one),
            vmem(BF16, n_blk, mine, subs * inner_rows, slots_one),
            vmem(F32, n_blk, subs, inner_rows, cols),
            vmem(F32, n_blk, subs, inner_rows, cols),
            vmem(BF16, slots, cols),
            vmem(BF16, subs, tile, slots_one),
            vmem(BF16, *coupling.shape),
            vmem(jnp.int32, *peer_device.shape),
            vmem(jnp.int32, *peer_lane.shape),
            pltpu.SMEM(blocks.shape, jnp.int32),
            sem((subs + 1,)),
            sem((5,)),
            sem((subs, 2)),
            sem((subs, 2, 2)),
            sem((subs, 2, 2)),
            sem((subs, mine, 2, 2)),
            sem((subs, mine, 2)),
            sem((2,)),
            sem((mine, 2)),
            sem((2,)),
            sem((3, 2)),
            sem((3, 2)),
        ],
        compiler_params=pltpu.CompilerParams(
            collective_id=0, has_side_effects=True, vmem_limit_bytes=56 * 1024 * 1024
        ),
        cost_estimate=pl.CostEstimate(
            flops=flops, bytes_accessed=2 * factor.size, transcendentals=0
        ),
    )(factor, samples, jnp.swapaxes(diagonal, 1, 2), coupling, blocks, peer_device, peer_lane).astype(BF16)


def solution(mesh):
    placed = (
        P("sub", None, "blk"),
        P("sub", "blk", None),
        P("sub", None, None),
        P("sub", "blk", None),
        P("sub"),
        P("sub", None),
        P("sub", None),
        P("sub", None),
    )
    return jax.shard_map(
        local, mesh=mesh, in_specs=placed, out_specs=P("sub", "blk", None), check_vma=False
    )
```

```python
import functools

import jax
import jax.numpy as jnp
from jax import lax
from jax.experimental import pallas as pl
from jax.experimental.pallas import tpu as pltpu
from jax.sharding import PartitionSpec as P

FACE_HALF = 104
MESH = pl.DeviceIdType.MESH
F32, BF16 = jnp.float32, jnp.bfloat16


def kernel(
    n_sub, n_blk, pad, main, extra,
    factor, samples, diagonal, coupling, blocks_in, peer_in, lane_in_ref, out,
    fac, drv, tr, parts, near, far, mixed, kept, diag_out, diag_in, main_out, main_in,
    tail_out, tail_in, coup_t, coup_out, coup_in, inner, diag_own,
    diag_raw, coup, peer_device, peer_lane, blocks,
    local_sem, small_sem, near_sem, far_sem, relay_sem, near_sum, far_sum, diag_sem, main_sem,
    tail_sem, coup_sem, last_sem,
):
    me, here = lax.axis_index("sub"), lax.axis_index("blk")
    subs, order, quarter = fac.shape
    tile, slots_one = diagonal.shape[1], diagonal.shape[2]
    slots = subs * slots_one
    cols = samples.shape[2]
    mine = tile // n_blk
    inner_rows = coupling.shape[1]
    twin = here + 1 - 2 * lax.rem(here, 2)
    cross = lax.rem(here + 2, n_blk)
    diag = lax.rem(twin + 2, n_blk)

    def remote(src, dst, sems, where):
        return pltpu.make_async_remote_copy(
            src_ref=src, dst_ref=dst, send_sem=sems.at[0], recv_sem=sems.at[1],
            device_id=where, device_id_type=MESH,
        )

    def sub_peer(step):
        return lax.rem(me + step, n_sub)

    barrier = pltpu.get_barrier_semaphore()
    for b in (twin, cross, diag):
        pl.semaphore_signal(barrier, inc=1, device_id={"blk": b}, device_id_type=MESH)

    def greet(step, carry):
        pl.semaphore_signal(
            barrier, inc=1, device_id={"sub": sub_peer(step)}, device_id_type=MESH
        )
        return carry

    lax.fori_loop(1, n_sub, greet, 0)

    small = [
        pltpu.make_async_copy(src, dst, small_sem.at[i])
        for i, (src, dst) in enumerate((
            (blocks_in, blocks), (peer_in, peer_device), (lane_in_ref, peer_lane),
            (diagonal, diag_raw), (coupling, coup),
        ))
    ]
    for c in small:
        c.start()
    own = pltpu.make_async_copy(samples, drv.at[here], local_sem.at[subs])
    own.start()
    load = []
    for s in range(subs):
        one = pltpu.make_async_copy(factor.at[s], fac.at[s], local_sem.at[s])
        one.start()
        load.append(one)

    pl.semaphore_wait(barrier, n_sub - 1 + 3)

    to_far = [
        remote(samples.at[s], drv.at[here, s], far_sem.at[s], {"blk": cross}) for s in range(subs)
    ]
    to_near = [
        remote(samples.at[s], drv.at[here, s], near_sem.at[s], {"blk": twin}) for s in range(subs)
    ]
    for s in range(subs):
        to_far[s].start()
    for s in range(subs):
        to_near[s].start()

    for c in small:
        c.wait()
    slot_of = lax.broadcasted_iota(jnp.int32, (1, slots_one), 1)
    peer_rows, peer_cols, lane_cols = [], [], []
    for s in range(subs):
        peer = jnp.where(slot_of < blocks[s], peer_device[pl.ds(s, 1), :], -1)
        peer_rows.append(peer)
        square = (slots_one, slots_one)
        peer_cols.append(jnp.broadcast_to(peer.astype(F32), square).T[:, :1])
        lanes = peer_lane[pl.ds(s, 1), :].astype(F32)
        lane_cols.append(jnp.broadcast_to(lanes, square).T[:, :1])
    peer_row = jnp.concatenate(peer_rows, axis=1)
    lane_row = jnp.concatenate([peer_lane[pl.ds(s, 1), :] for s in range(subs)], axis=1)
    peer_col = jnp.concatenate(peer_cols, axis=0).astype(jnp.int32)
    lane_col = jnp.concatenate(lane_cols, axis=0).astype(jnp.int32)
    live = peer_col >= 0
    inside = peer_col == me

    def target(peer, lane, size, low, high, offset):
        chosen = (peer >= 0) & (lane >= low) & (lane < high)
        return jnp.where(chosen, peer * size + (lane - low) + offset, -1)

    def place(size, low, high, offset=0):
        row_of = lax.broadcasted_iota(jnp.int32, (n_sub * size, slots), 0)
        wanted = target(peer_row, lane_row, size, low, high, offset)
        return jnp.where(row_of == wanted, 1.0, 0.0).astype(BF16)

    def collect(size, low, high, offset=0):
        lane_of = lax.broadcasted_iota(jnp.int32, (slots, n_sub * size), 1)
        wanted = target(peer_col, lane_col, size, low, high, offset)
        return jnp.where(lane_of == wanted, 1.0, 0.0).astype(BF16)

    def rows_of(index, size):
        return pl.ds(pl.multiple_of(index * size, 16), size)

    def send_faces(value, sent, got, sems, size):
        sent[...] = value.astype(BF16)
        got[rows_of(me, size), :] = sent[rows_of(me, size), :]

        def go(step, carry):
            remote(
                sent.at[rows_of(sub_peer(step), size)], got.at[rows_of(me, size)], sems,
                {"sub": sub_peer(step)},
            ).start()
            return carry

        lax.fori_loop(1, n_sub, go, 0)

    def wait_faces(sent, got, sems, size):
        every = pl.ds(0, (n_sub - 1) * size)
        remote(sent.at[every], got.at[every], sems, {"sub": sub_peer(1)}).wait()

    def dot(left, right):
        return jnp.dot(left, right, preferred_element_type=F32)

    for s in range(subs):
        wide = jnp.concatenate(
            [diag_raw[s].astype(F32), jnp.zeros((cols - tile, slots_one), F32)], axis=0
        )
        diag_own[s * slots_one:(s + 1) * slots_one, :] = wide.T.astype(BF16)
    send_faces(dot(place(pad, 0, pad), diag_own[...]), diag_out, diag_in, diag_sem, pad)

    own.wait()
    row_in = lax.broadcasted_iota(jnp.int32, (quarter, 1), 0)
    lane_in = lax.broadcasted_iota(jnp.int32, (1, quarter), 1)

    def first(s, b):
        begin = pl.multiple_of(b * quarter, quarter)
        rows_live = row_in + begin < blocks[s] * tile
        value = drv[b, s]
        value = jnp.where(rows_live, value, jnp.zeros_like(value))
        return lax.dot_general(
            value, fac[s, pl.ds(begin, quarter), :], (((0,), (0,)), ((), ())),
            preferred_element_type=F32,
        )

    near_copies, far_copies = {}, {}

    def send_near(s):
        span = pl.ds(s * slots_one, slots_one)
        for j, group in ((1, diag), (0, twin)):
            for k in range(mine):
                c = remote(
                    parts.at[group * mine + k, span], near.at[k, j, span],
                    near_sum.at[s, k, j], {"blk": twin},
                )
                c.start()
                near_copies[s, k, j] = c

    def send_far(s):
        span = pl.ds(s * slots_one, slots_one)
        for k in range(mine):
            near_copies[s, k, 1].wait()
            mixed[k, span, :] = (
                parts[cross * mine + k, span, :].astype(F32) + near[k, 1, span, :].astype(F32)
            ).astype(BF16)
            c = remote(mixed.at[k, span], far.at[k, span], far_sum.at[s, k], {"blk": cross})
            c.start()
            far_copies[s, k] = c

    for s in range(subs):
        load[s].wait()
        reduced = first(s, here)
        to_near[s].wait()
        reduced += first(s, twin)
        to_far[s].wait()
        relay = remote(drv.at[cross, s], drv.at[cross, s], relay_sem.at[s], {"blk": twin})
        relay.start()
        reduced += first(s, cross)
        if s:
            send_far(s - 1)
        relay.wait()
        reduced += first(s, diag)
        alive = lane_in + here * quarter < blocks[s] * tile
        reduced = jnp.where(alive, reduced, 0.0).astype(BF16)
        for q in range(0, order, quarter):
            tr[s, q:q + quarter, :] = lax.dot_general(
                fac[s, q:q + quarter, :], reduced, (((1,), (1,)), ((), ())),
                preferred_element_type=F32,
            )
        for t in range(tile):
            parts[t, s * slots_one:(s + 1) * slots_one, :] = tr[
                s, pl.ds(t, slots_one, stride=tile), :
            ].astype(BF16)
        send_near(s)
    send_far(subs - 1)

    tail = None
    for k in range(mine):
        for s in range(subs):
            near_copies[s, k, 0].wait()
            far_copies[s, k].wait()
        kept[k] = (
            parts[here * mine + k].astype(F32) + near[k, 0].astype(F32) + far[k].astype(F32)
        ).astype(BF16)
        if main:
            send_faces(
                dot(place(main, 0, main), kept[k]), main_out.at[k], main_in.at[k], main_sem.at[k],
                main,
            )
        if extra:
            got = dot(place(extra, main, pad, k * (extra // mine)), kept[k])
            tail = got if k == 0 else tail + got
    if extra:
        send_faces(tail, tail_out, tail_in, tail_sem, extra)

    wide = coup[...].reshape(subs * inner_rows, order).astype(F32)
    filler = jnp.zeros((coup_t.shape[1] - subs * inner_rows, order), F32)
    coup_t[...] = jnp.concatenate([wide, filler], axis=0).T
    for t in range(tile):
        piece = coup_t[pl.ds(t, slots_one, stride=tile), :].T
        coup_out[t] = piece[:subs * inner_rows].astype(BF16)
    coup_in[here] = coup_out[pl.ds(here * mine, mine)]
    coup_copies = [
        remote(coup_out.at[pl.ds(b * mine, mine)], coup_in.at[here], coup_sem.at[i], {"blk": b})
        for i, b in enumerate((twin, cross, diag))
    ]
    for c in coup_copies:
        c.start()

    def own_side(value):
        return jnp.where(inside, 0.0, value.astype(F32))

    wait_faces(diag_out, diag_in, diag_sem, pad)
    divisors = own_side(diag_own[...]) + dot(collect(pad, 0, pad), diag_in[...])
    lane_t = lax.broadcasted_iota(jnp.int32, (slots, cols), 1)
    divisor = []
    for k in range(mine):
        one = jnp.sum(jnp.where(lane_t == here * mine + k, divisors, 0.0), axis=1, keepdims=True)
        divisor.append(jnp.where(live, one, 1.0))
    for c in coup_copies:
        c.wait()
    total = []
    for k in range(mine):
        both = own_side(kept[k])
        if main:
            wait_faces(main_out.at[k], main_in.at[k], main_sem.at[k], main)
            both += dot(collect(main, 0, main), main_in[k])
        total.append(both)
    if extra:
        every = jnp.concatenate(
            [collect(extra, main, pad, k * (extra // mine)) for k in range(mine)], axis=0
        )
        wait_faces(tail_out, tail_in, tail_sem, extra)
        rest = dot(every, tail_in[...])
        for k in range(mine):
            total[k] += rest[k * slots:(k + 1) * slots]
    coefs = [
        jnp.where(live, total[k] / divisor[k], 0.0).astype(BF16) for k in range(mine)
    ]
    for s in range(subs):
        left = [
            coup_in[:, k, s * inner_rows:(s + 1) * inner_rows, :].reshape(
                n_blk * inner_rows, slots_one
            )
            for k in range(mine)
        ]
        right = [coef[s * slots_one:(s + 1) * slots_one] for coef in coefs]
        got = dot(jnp.concatenate(left, axis=1), jnp.concatenate(right, axis=0))
        inner[:, s] = got.reshape(n_blk, inner_rows, cols)
    last = [
        remote(inner.at[b], out.at[here], last_sem.at[i], {"blk": b})
        for i, b in enumerate((twin, cross, diag))
    ]
    for c in last:
        c.start()
    stay = pltpu.make_async_copy(inner.at[here], out.at[here], local_sem.at[subs])
    stay.start()
    stay.wait()
    for c in last:
        c.wait()


def local(factor, samples, diagonal, coupling, blocks, peer_device, peer_lane, owns_face):
    n_sub, n_blk = lax.axis_size("sub"), lax.axis_size("blk")
    subs, order, quarter = factor.shape
    slots_one, tile = diagonal.shape[1], diagonal.shape[2]
    slots, cols = subs * slots_one, samples.shape[2]
    mine, inner_rows = tile // n_blk, coupling.shape[1]
    half_cycle = (n_sub - 1) // 2
    capacity = (FACE_HALF + half_cycle - 1) // half_cycle
    pad = -(-capacity // 16) * 16
    main = capacity // 16 * 16
    extra = -(-(capacity - main) * mine // 16) * 16
    flops = 4 * subs * order * quarter * cols
    hbm = pl.BlockSpec(memory_space=pltpu.HBM)
    sem = pltpu.SemaphoreType.DMA
    coup_lanes = -(-subs * inner_rows // 128) * 128

    def vmem(kind, *dims):
        return pltpu.VMEM(tuple(max(d, 1) for d in dims), kind)

    shares = pl.pallas_call(
        functools.partial(kernel, n_sub, n_blk, pad, main, extra),
        out_shape=jax.ShapeDtypeStruct((n_blk, subs, inner_rows, cols), F32),
        in_specs=[hbm] * 7,
        out_specs=hbm,
        scratch_shapes=[
            vmem(BF16, subs, order, quarter),
            vmem(BF16, n_blk, subs, quarter, cols),
            vmem(F32, subs, order, cols),
            vmem(BF16, tile, slots, cols),
            vmem(BF16, mine, 2, slots, cols),
            vmem(BF16, mine, slots, cols),
            vmem(BF16, mine, slots, cols),
            vmem(BF16, mine, slots, cols),
            vmem(BF16, n_sub * pad, cols),
            vmem(BF16, n_sub * pad, cols),
            vmem(BF16, mine, n_sub * main, cols),
            vmem(BF16, mine, n_sub * main, cols),
            vmem(BF16, n_sub * extra, cols),
            vmem(BF16, n_sub * extra, cols),
            vmem(F32, order, coup_lanes),
            vmem(BF16, tile, subs * inner_rows, slots_one),
            vmem(BF16, n_blk, mine, subs * inner_rows, slots_one),
            vmem(F32, n_blk, subs, inner_rows, cols),
            vmem(BF16, slots, cols),
            vmem(BF16, subs, tile, slots_one),
            vmem(BF16, *coupling.shape),
            vmem(jnp.int32, *peer_device.shape),
            vmem(jnp.int32, *peer_lane.shape),
            pltpu.SMEM(blocks.shape, jnp.int32),
            sem((subs + 1,)),
            sem((5,)),
            sem((subs, 2)),
            sem((subs, 2)),
            sem((subs, 2)),
            sem((subs, mine, 2, 2)),
            sem((subs, mine, 2)),
            sem((2,)),
            sem((mine, 2)),
            sem((2,)),
            sem((3, 2)),
            sem((3, 2)),
        ],
        compiler_params=pltpu.CompilerParams(
            collective_id=0, has_side_effects=True, vmem_limit_bytes=56 * 1024 * 1024
        ),
        cost_estimate=pl.CostEstimate(
            flops=flops, bytes_accessed=2 * factor.size, transcendentals=0
        ),
    )(factor, samples, jnp.swapaxes(diagonal, 1, 2), coupling, blocks, peer_device, peer_lane)
    return jnp.sum(shares, axis=0).astype(BF16)


def solution(mesh):
    placed = (
        P("sub", None, "blk"),
        P("sub", "blk", None),
        P("sub", None, None),
        P("sub", "blk", None),
        P("sub"),
        P("sub", None),
        P("sub", None),
        P("sub", None),
    )
    return jax.shard_map(
        local, mesh=mesh, in_specs=placed, out_specs=P("sub", "blk", None), check_vma=False
    )
```

```python
import functools

import jax
import jax.numpy as jnp
from jax import lax
from jax.experimental import pallas as pl
from jax.experimental.pallas import tpu as pltpu
from jax.sharding import PartitionSpec as P

FACE_HALF = 104
MESH = pl.DeviceIdType.MESH
F32, BF16 = jnp.float32, jnp.bfloat16


def kernel(
    n_sub, n_blk, pad, main, extra,
    factor, samples, diagonal, coupling, blocks_in, peer_in, lane_in_ref, out,
    fac, drv, tr, parts, near, far, mixed, kept, diag_out, diag_in, main_out, main_in,
    tail_out, tail_in, coup_t, coup_out, coup_in, inner, diag_own,
    diag_raw, coup, peer_device, peer_lane, blocks,
    local_sem, small_sem, near_sem, far_sem, relay_sem, near_sum, far_sum, diag_sem, main_sem,
    tail_sem, coup_sem, last_sem,
):
    me, here = lax.axis_index("sub"), lax.axis_index("blk")
    subs, order, quarter = fac.shape
    tile, slots_one = diagonal.shape[1], diagonal.shape[2]
    slots = subs * slots_one
    cols = samples.shape[2]
    mine = tile // n_blk
    inner_rows = coupling.shape[1]
    twin = here + 1 - 2 * lax.rem(here, 2)
    cross = lax.rem(here + 2, n_blk)
    diag = lax.rem(twin + 2, n_blk)

    def remote(src, dst, sems, where):
        return pltpu.make_async_remote_copy(
            src_ref=src, dst_ref=dst, send_sem=sems.at[0], recv_sem=sems.at[1],
            device_id=where, device_id_type=MESH,
        )

    def sub_peer(step):
        return lax.rem(me + step, n_sub)

    barrier = pltpu.get_barrier_semaphore()

    def greet(step, carry):
        pl.semaphore_signal(
            barrier, inc=1, device_id={"sub": sub_peer(step)}, device_id_type=MESH
        )
        return carry

    lax.fori_loop(1, n_sub, greet, 0)
    for b in (diag, cross, twin):
        pl.semaphore_signal(barrier, inc=1, device_id={"blk": b}, device_id_type=MESH)

    small = [
        pltpu.make_async_copy(src, dst, small_sem.at[i])
        for i, (src, dst) in enumerate((
            (blocks_in, blocks), (peer_in, peer_device), (lane_in_ref, peer_lane),
            (diagonal, diag_raw), (coupling, coup),
        ))
    ]
    for c in small:
        c.start()
    own = pltpu.make_async_copy(samples, drv.at[here], local_sem.at[subs])
    own.start()
    load = []
    for s in range(subs):
        one = pltpu.make_async_copy(factor.at[s], fac.at[s], local_sem.at[s])
        one.start()
        load.append(one)

    pl.semaphore_wait(barrier, n_sub - 1 + 3)

    to_far = [
        remote(samples.at[s], drv.at[here, s], far_sem.at[s], {"blk": cross}) for s in range(subs)
    ]
    to_near = [
        remote(samples.at[s], drv.at[here, s], near_sem.at[s], {"blk": twin}) for s in range(subs)
    ]
    for s in range(subs):
        to_far[s].start()
    for s in range(subs):
        to_near[s].start()

    for c in small:
        c.wait()
    slot_of = lax.broadcasted_iota(jnp.int32, (1, slots_one), 1)
    peer_rows, peer_cols, lane_cols = [], [], []
    for s in range(subs):
        peer = jnp.where(slot_of < blocks[s], peer_device[pl.ds(s, 1), :], -1)
        peer_rows.append(peer)
        square = (slots_one, slots_one)
        peer_cols.append(jnp.broadcast_to(peer.astype(F32), square).T[:, :1])
        lanes = peer_lane[pl.ds(s, 1), :].astype(F32)
        lane_cols.append(jnp.broadcast_to(lanes, square).T[:, :1])
    peer_row = jnp.concatenate(peer_rows, axis=1)
    lane_row = jnp.concatenate([peer_lane[pl.ds(s, 1), :] for s in range(subs)], axis=1)
    peer_col = jnp.concatenate(peer_cols, axis=0).astype(jnp.int32)
    lane_col = jnp.concatenate(lane_cols, axis=0).astype(jnp.int32)
    live = peer_col >= 0
    inside = peer_col == me

    def target(peer, lane, size, low, high, offset):
        chosen = (peer >= 0) & (lane >= low) & (lane < high)
        return jnp.where(chosen, peer * size + (lane - low) + offset, -1)

    def place(size, low, high, offset=0):
        row_of = lax.broadcasted_iota(jnp.int32, (n_sub * size, slots), 0)
        wanted = target(peer_row, lane_row, size, low, high, offset)
        return jnp.where(row_of == wanted, 1.0, 0.0).astype(BF16)

    def collect(size, low, high, offset=0):
        lane_of = lax.broadcasted_iota(jnp.int32, (slots, n_sub * size), 1)
        wanted = target(peer_col, lane_col, size, low, high, offset)
        return jnp.where(lane_of == wanted, 1.0, 0.0).astype(BF16)

    def rows_of(index, size):
        return pl.ds(pl.multiple_of(index * size, 16), size)

    def send_faces(value, sent, got, sems, size):
        sent[...] = value.astype(BF16)
        got[rows_of(me, size), :] = sent[rows_of(me, size), :]

        def go(step, carry):
            remote(
                sent.at[rows_of(sub_peer(step), size)], got.at[rows_of(me, size)], sems,
                {"sub": sub_peer(step)},
            ).start()
            return carry

        lax.fori_loop(1, n_sub, go, 0)

    def wait_faces(sent, got, sems, size):
        every = pl.ds(0, (n_sub - 1) * size)
        remote(sent.at[every], got.at[every], sems, {"sub": sub_peer(1)}).wait()

    def dot(left, right):
        return jnp.dot(left, right, preferred_element_type=F32)

    for s in range(subs):
        wide = jnp.concatenate(
            [diag_raw[s].astype(F32), jnp.zeros((cols - tile, slots_one), F32)], axis=0
        )
        diag_own[s * slots_one:(s + 1) * slots_one, :] = wide.T.astype(BF16)
    send_faces(dot(place(pad, 0, pad), diag_own[...]), diag_out, diag_in, diag_sem, pad)

    own.wait()
    row_in = lax.broadcasted_iota(jnp.int32, (quarter, 1), 0)
    lane_in = lax.broadcasted_iota(jnp.int32, (1, quarter), 1)

    def first(s, b):
        begin = pl.multiple_of(b * quarter, quarter)
        rows_live = row_in + begin < blocks[s] * tile
        value = drv[b, s]
        value = jnp.where(rows_live, value, jnp.zeros_like(value))
        return lax.dot_general(
            value, fac[s, pl.ds(begin, quarter), :], (((0,), (0,)), ((), ())),
            preferred_element_type=F32,
        )

    near_copies, far_copies = {}, {}

    def send_near(s):
        span = pl.ds(s * slots_one, slots_one)
        for j, group in ((1, diag), (0, twin)):
            for k in range(mine):
                c = remote(
                    parts.at[group * mine + k, span], near.at[k, j, span],
                    near_sum.at[s, k, j], {"blk": twin},
                )
                c.start()
                near_copies[s, k, j] = c

    def send_far(s):
        span = pl.ds(s * slots_one, slots_one)
        for k in range(mine):
            near_copies[s, k, 1].wait()
            mixed[k, span, :] = (
                parts[cross * mine + k, span, :].astype(F32) + near[k, 1, span, :].astype(F32)
            ).astype(BF16)
            c = remote(mixed.at[k, span], far.at[k, span], far_sum.at[s, k], {"blk": cross})
            c.start()
            far_copies[s, k] = c

    def begin_sub(s):
        load[s].wait()
        held = first(s, here)
        to_near[s].wait()
        return held + first(s, twin)

    later = begin_sub(0)
    for s in range(subs):
        reduced = later
        to_far[s].wait()
        relay = remote(drv.at[cross, s], drv.at[cross, s], relay_sem.at[s], {"blk": twin})
        relay.start()
        reduced += first(s, cross)
        if s:
            send_far(s - 1)
        if s + 1 < subs:
            later = begin_sub(s + 1)
        relay.wait()
        reduced += first(s, diag)
        alive = lane_in + here * quarter < blocks[s] * tile
        reduced = jnp.where(alive, reduced, 0.0).astype(BF16)
        for q in range(0, order, quarter):
            tr[s, q:q + quarter, :] = lax.dot_general(
                fac[s, q:q + quarter, :], reduced, (((1,), (1,)), ((), ())),
                preferred_element_type=F32,
            )
        for t in range(tile):
            parts[t, s * slots_one:(s + 1) * slots_one, :] = tr[
                s, pl.ds(t, slots_one, stride=tile), :
            ].astype(BF16)
        send_near(s)
    send_far(subs - 1)

    tail = None
    for k in range(mine):
        for s in range(subs):
            near_copies[s, k, 0].wait()
            far_copies[s, k].wait()
        kept[k] = (
            parts[here * mine + k].astype(F32) + near[k, 0].astype(F32) + far[k].astype(F32)
        ).astype(BF16)
        if main:
            send_faces(
                dot(place(main, 0, main), kept[k]), main_out.at[k], main_in.at[k], main_sem.at[k],
                main,
            )
        if extra:
            got = dot(place(extra, main, pad, k * (extra // mine)), kept[k])
            tail = got if k == 0 else tail + got
    if extra:
        send_faces(tail, tail_out, tail_in, tail_sem, extra)

    wide = coup[...].reshape(subs * inner_rows, order).astype(F32)
    filler = jnp.zeros((coup_t.shape[1] - subs * inner_rows, order), F32)
    coup_t[...] = jnp.concatenate([wide, filler], axis=0).T
    for t in range(tile):
        piece = coup_t[pl.ds(t, slots_one, stride=tile), :].T
        coup_out[t] = piece[:subs * inner_rows].astype(BF16)
    coup_in[here] = coup_out[pl.ds(here * mine, mine)]
    coup_copies = [
        remote(coup_out.at[pl.ds(b * mine, mine)], coup_in.at[here], coup_sem.at[i], {"blk": b})
        for i, b in enumerate((twin, cross, diag))
    ]
    for c in coup_copies:
        c.start()

    def own_side(value):
        return jnp.where(inside, 0.0, value.astype(F32))

    wait_faces(diag_out, diag_in, diag_sem, pad)
    divisors = own_side(diag_own[...]) + dot(collect(pad, 0, pad), diag_in[...])
    lane_t = lax.broadcasted_iota(jnp.int32, (slots, cols), 1)
    divisor = []
    for k in range(mine):
        one = jnp.sum(jnp.where(lane_t == here * mine + k, divisors, 0.0), axis=1, keepdims=True)
        divisor.append(jnp.where(live, one, 1.0))
    for c in coup_copies:
        c.wait()
    total = []
    for k in range(mine):
        both = own_side(kept[k])
        if main:
            wait_faces(main_out.at[k], main_in.at[k], main_sem.at[k], main)
            both += dot(collect(main, 0, main), main_in[k])
        total.append(both)
    if extra:
        every = jnp.concatenate(
            [collect(extra, main, pad, k * (extra // mine)) for k in range(mine)], axis=0
        )
        wait_faces(tail_out, tail_in, tail_sem, extra)
        rest = dot(every, tail_in[...])
        for k in range(mine):
            total[k] += rest[k * slots:(k + 1) * slots]
    coefs = [
        jnp.where(live, total[k] / divisor[k], 0.0).astype(BF16) for k in range(mine)
    ]
    for s in range(subs):
        left = [
            coup_in[:, k, s * inner_rows:(s + 1) * inner_rows, :].reshape(
                n_blk * inner_rows, slots_one
            )
            for k in range(mine)
        ]
        right = [coef[s * slots_one:(s + 1) * slots_one] for coef in coefs]
        got = dot(jnp.concatenate(left, axis=1), jnp.concatenate(right, axis=0))
        inner[:, s] = got.reshape(n_blk, inner_rows, cols)
    last = [
        remote(inner.at[b], out.at[here], last_sem.at[i], {"blk": b})
        for i, b in enumerate((twin, cross, diag))
    ]
    for c in last:
        c.start()
    stay = pltpu.make_async_copy(inner.at[here], out.at[here], local_sem.at[subs])
    stay.start()
    stay.wait()
    for c in last:
        c.wait()


def local(factor, samples, diagonal, coupling, blocks, peer_device, peer_lane, owns_face):
    n_sub, n_blk = lax.axis_size("sub"), lax.axis_size("blk")
    subs, order, quarter = factor.shape
    slots_one, tile = diagonal.shape[1], diagonal.shape[2]
    slots, cols = subs * slots_one, samples.shape[2]
    mine, inner_rows = tile // n_blk, coupling.shape[1]
    half_cycle = (n_sub - 1) // 2
    capacity = (FACE_HALF + half_cycle - 1) // half_cycle
    pad = -(-capacity // 16) * 16
    main = capacity // 16 * 16
    extra = -(-(capacity - main) * mine // 16) * 16
    flops = 4 * subs * order * quarter * cols
    hbm = pl.BlockSpec(memory_space=pltpu.HBM)
    sem = pltpu.SemaphoreType.DMA
    coup_lanes = -(-subs * inner_rows // 128) * 128

    def vmem(kind, *dims):
        return pltpu.VMEM(tuple(max(d, 1) for d in dims), kind)

    shares = pl.pallas_call(
        functools.partial(kernel, n_sub, n_blk, pad, main, extra),
        out_shape=jax.ShapeDtypeStruct((n_blk, subs, inner_rows, cols), F32),
        in_specs=[hbm] * 7,
        out_specs=hbm,
        scratch_shapes=[
            vmem(BF16, subs, order, quarter),
            vmem(BF16, n_blk, subs, quarter, cols),
            vmem(F32, subs, order, cols),
            vmem(BF16, tile, slots, cols),
            vmem(BF16, mine, 2, slots, cols),
            vmem(BF16, mine, slots, cols),
            vmem(BF16, mine, slots, cols),
            vmem(BF16, mine, slots, cols),
            vmem(BF16, n_sub * pad, cols),
            vmem(BF16, n_sub * pad, cols),
            vmem(BF16, mine, n_sub * main, cols),
            vmem(BF16, mine, n_sub * main, cols),
            vmem(BF16, n_sub * extra, cols),
            vmem(BF16, n_sub * extra, cols),
            vmem(F32, order, coup_lanes),
            vmem(BF16, tile, subs * inner_rows, slots_one),
            vmem(BF16, n_blk, mine, subs * inner_rows, slots_one),
            vmem(F32, n_blk, subs, inner_rows, cols),
            vmem(BF16, slots, cols),
            vmem(BF16, subs, tile, slots_one),
            vmem(BF16, *coupling.shape),
            vmem(jnp.int32, *peer_device.shape),
            vmem(jnp.int32, *peer_lane.shape),
            pltpu.SMEM(blocks.shape, jnp.int32),
            sem((subs + 1,)),
            sem((5,)),
            sem((subs, 2)),
            sem((subs, 2)),
            sem((subs, 2)),
            sem((subs, mine, 2, 2)),
            sem((subs, mine, 2)),
            sem((2,)),
            sem((mine, 2)),
            sem((2,)),
            sem((3, 2)),
            sem((3, 2)),
        ],
        compiler_params=pltpu.CompilerParams(
            collective_id=0, has_side_effects=True, vmem_limit_bytes=56 * 1024 * 1024
        ),
        cost_estimate=pl.CostEstimate(
            flops=flops, bytes_accessed=2 * factor.size, transcendentals=0
        ),
    )(factor, samples, jnp.swapaxes(diagonal, 1, 2), coupling, blocks, peer_device, peer_lane)
    return jnp.sum(shares, axis=0).astype(BF16)


def solution(mesh):
    placed = (
        P("sub", None, "blk"),
        P("sub", "blk", None),
        P("sub", None, None),
        P("sub", "blk", None),
        P("sub"),
        P("sub", None),
        P("sub", None),
        P("sub", None),
    )
    return jax.shard_map(
        local, mesh=mesh, in_specs=placed, out_specs=P("sub", "blk", None), check_vma=False
    )
```

```python
import functools

import jax
import jax.numpy as jnp
from jax import lax
from jax.experimental import pallas as pl
from jax.experimental.pallas import tpu as pltpu
from jax.sharding import PartitionSpec as P

FACE_HALF = 104
MESH = pl.DeviceIdType.MESH
F32, BF16 = jnp.float32, jnp.bfloat16


def kernel(
    n_sub, n_blk, pad, main, extra,
    factor, samples, diagonal, coupling, blocks_in, peer_in, lane_in_ref, out,
    fac, drv, tr, parts, near, far, mixed, kept, diag_out, diag_in, main_out, main_in,
    tail_out, tail_in, coup_t, coup_out, coup_in, inner, diag_own,
    diag_raw, coup, peer_device, peer_lane, blocks,
    local_sem, small_sem, near_sem, far_sem, relay_sem, near_sum, far_sum, diag_sem, main_sem,
    tail_sem, coup_sem, last_sem,
):
    me, here = lax.axis_index("sub"), lax.axis_index("blk")
    subs, order, quarter = fac.shape
    tile, slots_one = diagonal.shape[1], diagonal.shape[2]
    slots = subs * slots_one
    cols = samples.shape[2]
    mine = tile // n_blk
    inner_rows = coupling.shape[1]
    twin = here + 1 - 2 * lax.rem(here, 2)
    cross = lax.rem(here + 2, n_blk)
    diag = lax.rem(twin + 2, n_blk)

    def remote(src, dst, sems, where):
        return pltpu.make_async_remote_copy(
            src_ref=src, dst_ref=dst, send_sem=sems.at[0], recv_sem=sems.at[1],
            device_id=where, device_id_type=MESH,
        )

    def sub_peer(step):
        return lax.rem(me + step, n_sub)

    barrier = pltpu.get_barrier_semaphore()

    def greet(step, carry):
        pl.semaphore_signal(
            barrier, inc=1, device_id={"sub": sub_peer(step)}, device_id_type=MESH
        )
        return carry

    lax.fori_loop(1, n_sub, greet, 0)
    for b in (diag, cross, twin):
        pl.semaphore_signal(barrier, inc=1, device_id={"blk": b}, device_id_type=MESH)

    small = [
        pltpu.make_async_copy(src, dst, small_sem.at[i])
        for i, (src, dst) in enumerate((
            (blocks_in, blocks), (peer_in, peer_device), (lane_in_ref, peer_lane),
            (diagonal, diag_raw), (coupling, coup),
        ))
    ]
    for c in small:
        c.start()
    own = pltpu.make_async_copy(samples, drv.at[here], local_sem.at[subs])
    own.start()
    load = []
    for s in range(subs):
        one = pltpu.make_async_copy(factor.at[s], fac.at[s], local_sem.at[s])
        one.start()
        load.append(one)

    pl.semaphore_wait(barrier, n_sub - 1 + 3)

    to_far = [
        remote(samples.at[s], drv.at[here, s], far_sem.at[s], {"blk": cross}) for s in range(subs)
    ]
    to_near = [
        remote(samples.at[s], drv.at[here, s], near_sem.at[s], {"blk": twin}) for s in range(subs)
    ]
    for s in range(subs):
        to_far[s].start()
    for s in range(subs):
        to_near[s].start()

    for c in small:
        c.wait()
    slot_of = lax.broadcasted_iota(jnp.int32, (1, slots_one), 1)
    peer_rows, peer_cols, lane_cols = [], [], []
    for s in range(subs):
        peer = jnp.where(slot_of < blocks[s], peer_device[pl.ds(s, 1), :], -1)
        peer_rows.append(peer)
        square = (slots_one, slots_one)
        peer_cols.append(jnp.broadcast_to(peer.astype(F32), square).T[:, :1])
        lanes = peer_lane[pl.ds(s, 1), :].astype(F32)
        lane_cols.append(jnp.broadcast_to(lanes, square).T[:, :1])
    peer_row = jnp.concatenate(peer_rows, axis=1)
    lane_row = jnp.concatenate([peer_lane[pl.ds(s, 1), :] for s in range(subs)], axis=1)
    peer_col = jnp.concatenate(peer_cols, axis=0).astype(jnp.int32)
    lane_col = jnp.concatenate(lane_cols, axis=0).astype(jnp.int32)
    live = peer_col >= 0
    inside = peer_col == me

    def target(peer, lane, size, low, high, offset):
        chosen = (peer >= 0) & (lane >= low) & (lane < high)
        return jnp.where(chosen, peer * size + (lane - low) + offset, -1)

    def place(size, low, high, offset=0):
        row_of = lax.broadcasted_iota(jnp.int32, (n_sub * size, slots), 0)
        wanted = target(peer_row, lane_row, size, low, high, offset)
        return jnp.where(row_of == wanted, 1.0, 0.0).astype(BF16)

    def collect(size, low, high, offset=0):
        lane_of = lax.broadcasted_iota(jnp.int32, (slots, n_sub * size), 1)
        wanted = target(peer_col, lane_col, size, low, high, offset)
        return jnp.where(lane_of == wanted, 1.0, 0.0).astype(BF16)

    def rows_of(index, size):
        return pl.ds(pl.multiple_of(index * size, 16), size)

    def send_faces(value, sent, got, sems, size):
        sent[...] = value.astype(BF16)
        got[rows_of(me, size), :] = sent[rows_of(me, size), :]

        def go(step, carry):
            remote(
                sent.at[rows_of(sub_peer(step), size)], got.at[rows_of(me, size)], sems,
                {"sub": sub_peer(step)},
            ).start()
            return carry

        lax.fori_loop(1, n_sub, go, 0)

    def wait_faces(sent, got, sems, size):
        every = pl.ds(0, (n_sub - 1) * size)
        remote(sent.at[every], got.at[every], sems, {"sub": sub_peer(1)}).wait()

    def dot(left, right):
        return jnp.dot(left, right, preferred_element_type=F32)

    for s in range(subs):
        wide = jnp.concatenate(
            [diag_raw[s].astype(F32), jnp.zeros((cols - tile, slots_one), F32)], axis=0
        )
        diag_own[s * slots_one:(s + 1) * slots_one, :] = wide.T.astype(BF16)
    send_faces(dot(place(pad, 0, pad), diag_own[...]), diag_out, diag_in, diag_sem, pad)

    own.wait()
    row_in = lax.broadcasted_iota(jnp.int32, (quarter, 1), 0)
    lane_in = lax.broadcasted_iota(jnp.int32, (1, quarter), 1)

    def first(s, b):
        begin = pl.multiple_of(b * quarter, quarter)
        rows_live = row_in + begin < blocks[s] * tile
        value = drv[b, s]
        value = jnp.where(rows_live, value, jnp.zeros_like(value))
        return lax.dot_general(
            value, fac[s, pl.ds(begin, quarter), :], (((0,), (0,)), ((), ())),
            preferred_element_type=F32,
        )

    near_copies, far_copies = {}, {}

    def send_near(s):
        span = pl.ds(s * slots_one, slots_one)
        for j, group in ((1, diag), (0, twin)):
            for k in range(mine):
                c = remote(
                    parts.at[group * mine + k, span], near.at[k, j, span],
                    near_sum.at[s, k, j], {"blk": twin},
                )
                c.start()
                near_copies[s, k, j] = c

    def send_far(s):
        span = pl.ds(s * slots_one, slots_one)
        for k in range(mine):
            near_copies[s, k, 1].wait()
            mixed[k, span, :] = (
                parts[cross * mine + k, span, :].astype(F32) + near[k, 1, span, :].astype(F32)
            ).astype(BF16)
            c = remote(mixed.at[k, span], far.at[k, span], far_sum.at[s, k], {"blk": cross})
            c.start()
            far_copies[s, k] = c

    def begin_sub(s):
        load[s].wait()
        held = first(s, here)
        to_near[s].wait()
        return held + first(s, twin)

    later = begin_sub(0)
    wide = coup[...].reshape(subs * inner_rows, order).astype(F32)
    filler = jnp.zeros((coup_t.shape[1] - subs * inner_rows, order), F32)
    coup_t[...] = jnp.concatenate([wide, filler], axis=0).T
    for s in range(subs):
        reduced = later
        to_far[s].wait()
        relay = remote(drv.at[cross, s], drv.at[cross, s], relay_sem.at[s], {"blk": twin})
        relay.start()
        reduced += first(s, cross)
        if s:
            send_far(s - 1)
        if s + 1 < subs:
            later = begin_sub(s + 1)
        relay.wait()
        reduced += first(s, diag)
        alive = lane_in + here * quarter < blocks[s] * tile
        reduced = jnp.where(alive, reduced, 0.0).astype(BF16)
        for q in range(0, order, quarter):
            tr[s, q:q + quarter, :] = lax.dot_general(
                fac[s, q:q + quarter, :], reduced, (((1,), (1,)), ((), ())),
                preferred_element_type=F32,
            )
        for t in range(tile):
            parts[t, s * slots_one:(s + 1) * slots_one, :] = tr[
                s, pl.ds(t, slots_one, stride=tile), :
            ].astype(BF16)
        send_near(s)
    send_far(subs - 1)

    tail = None
    for k in range(mine):
        for s in range(subs):
            near_copies[s, k, 0].wait()
            far_copies[s, k].wait()
        kept[k] = (
            parts[here * mine + k].astype(F32) + near[k, 0].astype(F32) + far[k].astype(F32)
        ).astype(BF16)
        if main:
            send_faces(
                dot(place(main, 0, main), kept[k]), main_out.at[k], main_in.at[k], main_sem.at[k],
                main,
            )
        if extra:
            got = dot(place(extra, main, pad, k * (extra // mine)), kept[k])
            tail = got if k == 0 else tail + got
    if extra:
        send_faces(tail, tail_out, tail_in, tail_sem, extra)

    for t in range(tile):
        piece = coup_t[pl.ds(t, slots_one, stride=tile), :].T
        coup_out[t] = piece[:subs * inner_rows].astype(BF16)
    coup_in[here] = coup_out[pl.ds(here * mine, mine)]
    coup_copies = [
        remote(coup_out.at[pl.ds(b * mine, mine)], coup_in.at[here], coup_sem.at[i], {"blk": b})
        for i, b in enumerate((twin, cross, diag))
    ]
    for c in coup_copies:
        c.start()

    def own_side(value):
        return jnp.where(inside, 0.0, value.astype(F32))

    wait_faces(diag_out, diag_in, diag_sem, pad)
    divisors = own_side(diag_own[...]) + dot(collect(pad, 0, pad), diag_in[...])
    lane_t = lax.broadcasted_iota(jnp.int32, (slots, cols), 1)
    divisor = []
    for k in range(mine):
        one = jnp.sum(jnp.where(lane_t == here * mine + k, divisors, 0.0), axis=1, keepdims=True)
        divisor.append(jnp.where(live, one, 1.0))
    total = []
    for k in range(mine):
        both = own_side(kept[k])
        if main:
            wait_faces(main_out.at[k], main_in.at[k], main_sem.at[k], main)
            both += dot(collect(main, 0, main), main_in[k])
        total.append(both)
    if extra:
        every = jnp.concatenate(
            [collect(extra, main, pad, k * (extra // mine)) for k in range(mine)], axis=0
        )
        wait_faces(tail_out, tail_in, tail_sem, extra)
        rest = dot(every, tail_in[...])
        for k in range(mine):
            total[k] += rest[k * slots:(k + 1) * slots]
    for c in coup_copies:
        c.wait()
    coefs = [
        jnp.where(live, total[k] / divisor[k], 0.0).astype(BF16) for k in range(mine)
    ]
    for s in range(subs):
        left = [
            coup_in[:, k, s * inner_rows:(s + 1) * inner_rows, :].reshape(
                n_blk * inner_rows, slots_one
            )
            for k in range(mine)
        ]
        right = [coef[s * slots_one:(s + 1) * slots_one] for coef in coefs]
        got = dot(jnp.concatenate(left, axis=1), jnp.concatenate(right, axis=0))
        inner[:, s] = got.reshape(n_blk, inner_rows, cols)
    last = [
        remote(inner.at[b], out.at[here], last_sem.at[i], {"blk": b})
        for i, b in enumerate((twin, cross, diag))
    ]
    for c in last:
        c.start()
    stay = pltpu.make_async_copy(inner.at[here], out.at[here], local_sem.at[subs])
    stay.start()
    stay.wait()
    for c in last:
        c.wait()


def local(factor, samples, diagonal, coupling, blocks, peer_device, peer_lane, owns_face):
    n_sub, n_blk = lax.axis_size("sub"), lax.axis_size("blk")
    subs, order, quarter = factor.shape
    slots_one, tile = diagonal.shape[1], diagonal.shape[2]
    slots, cols = subs * slots_one, samples.shape[2]
    mine, inner_rows = tile // n_blk, coupling.shape[1]
    half_cycle = (n_sub - 1) // 2
    capacity = (FACE_HALF + half_cycle - 1) // half_cycle
    pad = -(-capacity // 16) * 16
    main = capacity // 16 * 16
    extra = -(-(capacity - main) * mine // 16) * 16
    flops = 4 * subs * order * quarter * cols
    hbm = pl.BlockSpec(memory_space=pltpu.HBM)
    sem = pltpu.SemaphoreType.DMA
    coup_lanes = -(-subs * inner_rows // 128) * 128

    def vmem(kind, *dims):
        return pltpu.VMEM(tuple(max(d, 1) for d in dims), kind)

    shares = pl.pallas_call(
        functools.partial(kernel, n_sub, n_blk, pad, main, extra),
        out_shape=jax.ShapeDtypeStruct((n_blk, subs, inner_rows, cols), F32),
        in_specs=[hbm] * 7,
        out_specs=hbm,
        scratch_shapes=[
            vmem(BF16, subs, order, quarter),
            vmem(BF16, n_blk, subs, quarter, cols),
            vmem(F32, subs, order, cols),
            vmem(BF16, tile, slots, cols),
            vmem(BF16, mine, 2, slots, cols),
            vmem(BF16, mine, slots, cols),
            vmem(BF16, mine, slots, cols),
            vmem(BF16, mine, slots, cols),
            vmem(BF16, n_sub * pad, cols),
            vmem(BF16, n_sub * pad, cols),
            vmem(BF16, mine, n_sub * main, cols),
            vmem(BF16, mine, n_sub * main, cols),
            vmem(BF16, n_sub * extra, cols),
            vmem(BF16, n_sub * extra, cols),
            vmem(F32, order, coup_lanes),
            vmem(BF16, tile, subs * inner_rows, slots_one),
            vmem(BF16, n_blk, mine, subs * inner_rows, slots_one),
            vmem(F32, n_blk, subs, inner_rows, cols),
            vmem(BF16, slots, cols),
            vmem(BF16, subs, tile, slots_one),
            vmem(BF16, *coupling.shape),
            vmem(jnp.int32, *peer_device.shape),
            vmem(jnp.int32, *peer_lane.shape),
            pltpu.SMEM(blocks.shape, jnp.int32),
            sem((subs + 1,)),
            sem((5,)),
            sem((subs, 2)),
            sem((subs, 2)),
            sem((subs, 2)),
            sem((subs, mine, 2, 2)),
            sem((subs, mine, 2)),
            sem((2,)),
            sem((mine, 2)),
            sem((2,)),
            sem((3, 2)),
            sem((3, 2)),
        ],
        compiler_params=pltpu.CompilerParams(
            collective_id=0, has_side_effects=True, vmem_limit_bytes=56 * 1024 * 1024
        ),
        cost_estimate=pl.CostEstimate(
            flops=flops, bytes_accessed=2 * factor.size, transcendentals=0
        ),
    )(factor, samples, jnp.swapaxes(diagonal, 1, 2), coupling, blocks, peer_device, peer_lane)
    return jnp.sum(shares, axis=0).astype(BF16)


def solution(mesh):
    placed = (
        P("sub", None, "blk"),
        P("sub", "blk", None),
        P("sub", None, None),
        P("sub", "blk", None),
        P("sub"),
        P("sub", None),
        P("sub", None),
        P("sub", None),
    )
    return jax.shard_map(
        local, mesh=mesh, in_specs=placed, out_specs=P("sub", "blk", None), check_vma=False
    )
```

```python
import functools

import jax
import jax.numpy as jnp
from jax import lax
from jax.experimental import pallas as pl
from jax.experimental.pallas import tpu as pltpu
from jax.sharding import PartitionSpec as P

FACE_HALF = 104
MESH = pl.DeviceIdType.MESH
F32, BF16 = jnp.float32, jnp.bfloat16


def kernel(
    n_sub, n_blk, pad, main, extra,
    factor, samples, diagonal, coupling, blocks_in, peer_in, lane_in_ref, out,
    fac, drv, tr, parts, near, far, mixed, kept, diag_out, diag_in, main_out, main_in,
    tail_out, tail_in, coup_t, coup_out, coup_in, inner, diag_own,
    diag_raw, coup, peer_device, peer_lane, blocks,
    local_sem, small_sem, near_sem, far_sem, relay_sem, near_sum, far_sum, diag_sem, main_sem,
    tail_sem, coup_sem, last_sem,
):
    me, here = lax.axis_index("sub"), lax.axis_index("blk")
    subs, order, quarter = fac.shape
    tile, slots_one = diagonal.shape[1], diagonal.shape[2]
    slots = subs * slots_one
    cols = samples.shape[2]
    mine = tile // n_blk
    inner_rows = coupling.shape[1]
    twin = here + 1 - 2 * lax.rem(here, 2)
    cross = lax.rem(here + 2, n_blk)
    diag = lax.rem(twin + 2, n_blk)

    def remote(src, dst, sems, where):
        return pltpu.make_async_remote_copy(
            src_ref=src, dst_ref=dst, send_sem=sems.at[0], recv_sem=sems.at[1],
            device_id=where, device_id_type=MESH,
        )

    def sub_peer(step):
        return lax.rem(me + step, n_sub)

    barrier = pltpu.get_barrier_semaphore()

    def greet(step, carry):
        pl.semaphore_signal(
            barrier, inc=1, device_id={"sub": sub_peer(step)}, device_id_type=MESH
        )
        return carry

    lax.fori_loop(1, n_sub, greet, 0)
    for b in (diag, cross, twin):
        pl.semaphore_signal(barrier, inc=1, device_id={"blk": b}, device_id_type=MESH)

    small = [
        pltpu.make_async_copy(src, dst, small_sem.at[i])
        for i, (src, dst) in enumerate((
            (blocks_in, blocks), (peer_in, peer_device), (lane_in_ref, peer_lane),
            (diagonal, diag_raw), (coupling, coup),
        ))
    ]
    for c in small:
        c.start()
    own = pltpu.make_async_copy(samples, drv.at[here], local_sem.at[subs])
    own.start()
    load = []
    for s in range(subs):
        one = pltpu.make_async_copy(factor.at[s], fac.at[s], local_sem.at[s])
        one.start()
        load.append(one)

    pl.semaphore_wait(barrier, n_sub - 1 + 3)

    to_far = [
        remote(samples.at[s], drv.at[here, s], far_sem.at[s], {"blk": cross}) for s in range(subs)
    ]
    to_near = [
        remote(samples.at[s], drv.at[here, s], near_sem.at[s], {"blk": twin}) for s in range(subs)
    ]
    for s in range(subs):
        to_far[s].start()
    for s in range(subs):
        to_near[s].start()

    for c in small:
        c.wait()
    slot_of = lax.broadcasted_iota(jnp.int32, (1, slots_one), 1)
    peer_rows, peer_cols, lane_cols = [], [], []
    for s in range(subs):
        peer = jnp.where(slot_of < blocks[s], peer_device[pl.ds(s, 1), :], -1)
        peer_rows.append(peer)
        square = (slots_one, slots_one)
        peer_cols.append(jnp.broadcast_to(peer.astype(F32), square).T[:, :1])
        lanes = peer_lane[pl.ds(s, 1), :].astype(F32)
        lane_cols.append(jnp.broadcast_to(lanes, square).T[:, :1])
    peer_row = jnp.concatenate(peer_rows, axis=1)
    lane_row = jnp.concatenate([peer_lane[pl.ds(s, 1), :] for s in range(subs)], axis=1)
    peer_col = jnp.concatenate(peer_cols, axis=0).astype(jnp.int32)
    lane_col = jnp.concatenate(lane_cols, axis=0).astype(jnp.int32)
    live = peer_col >= 0
    inside = peer_col == me

    def target(peer, lane, size, low, high, offset):
        chosen = (peer >= 0) & (lane >= low) & (lane < high)
        return jnp.where(chosen, peer * size + (lane - low) + offset, -1)

    def place(size, low, high, offset=0):
        row_of = lax.broadcasted_iota(jnp.int32, (n_sub * size, slots), 0)
        wanted = target(peer_row, lane_row, size, low, high, offset)
        return jnp.where(row_of == wanted, 1.0, 0.0).astype(BF16)

    def collect(size, low, high, offset=0):
        lane_of = lax.broadcasted_iota(jnp.int32, (slots, n_sub * size), 1)
        wanted = target(peer_col, lane_col, size, low, high, offset)
        return jnp.where(lane_of == wanted, 1.0, 0.0).astype(BF16)

    def rows_of(index, size):
        return pl.ds(pl.multiple_of(index * size, 16), size)

    def send_faces(value, sent, got, sems, size):
        sent[...] = value.astype(BF16)
        got[rows_of(me, size), :] = sent[rows_of(me, size), :]

        def go(step, carry):
            remote(
                sent.at[rows_of(sub_peer(step), size)], got.at[rows_of(me, size)], sems,
                {"sub": sub_peer(step)},
            ).start()
            return carry

        lax.fori_loop(1, n_sub, go, 0)

    def wait_faces(sent, got, sems, size):
        every = pl.ds(0, (n_sub - 1) * size)
        remote(sent.at[every], got.at[every], sems, {"sub": sub_peer(1)}).wait()

    def dot(left, right):
        return jnp.dot(left, right, preferred_element_type=F32)

    for s in range(subs):
        wide = jnp.concatenate(
            [diag_raw[s].astype(F32), jnp.zeros((cols - tile, slots_one), F32)], axis=0
        )
        diag_own[s * slots_one:(s + 1) * slots_one, :] = wide.T.astype(BF16)
    send_faces(dot(place(pad, 0, pad), diag_own[...]), diag_out, diag_in, diag_sem, pad)

    own.wait()
    row_in = lax.broadcasted_iota(jnp.int32, (quarter, 1), 0)
    lane_in = lax.broadcasted_iota(jnp.int32, (1, quarter), 1)

    def first(s, b):
        begin = pl.multiple_of(b * quarter, quarter)
        rows_live = row_in + begin < blocks[s] * tile
        value = drv[b, s]
        value = jnp.where(rows_live, value, jnp.zeros_like(value))
        return lax.dot_general(
            value, fac[s, pl.ds(begin, quarter), :], (((0,), (0,)), ((), ())),
            preferred_element_type=F32,
        )

    near_copies, far_copies = {}, {}

    def send_near(s):
        span = pl.ds(s * slots_one, slots_one)
        for j, group in ((1, diag), (0, twin)):
            for k in range(mine):
                c = remote(
                    parts.at[group * mine + k, span], near.at[k, j, span],
                    near_sum.at[s, k, j], {"blk": twin},
                )
                c.start()
                near_copies[s, k, j] = c

    def send_far(s):
        span = pl.ds(s * slots_one, slots_one)
        for k in range(mine):
            near_copies[s, k, 1].wait()
            mixed[k, span, :] = (
                parts[cross * mine + k, span, :].astype(F32) + near[k, 1, span, :].astype(F32)
            ).astype(BF16)
            c = remote(mixed.at[k, span], far.at[k, span], far_sum.at[s, k], {"blk": cross})
            c.start()
            far_copies[s, k] = c

    def begin_sub(s):
        load[s].wait()
        held = first(s, here)
        to_near[s].wait()
        return held + first(s, twin)

    later = begin_sub(0)
    for s in range(subs):
        reduced = later
        to_far[s].wait()
        relay = remote(drv.at[cross, s], drv.at[cross, s], relay_sem.at[s], {"blk": twin})
        relay.start()
        if s:
            send_far(s - 1)
        reduced += first(s, cross)
        if s + 1 < subs:
            later = begin_sub(s + 1)
        relay.wait()
        reduced += first(s, diag)
        alive = lane_in + here * quarter < blocks[s] * tile
        reduced = jnp.where(alive, reduced, 0.0).astype(BF16)
        for q in range(0, order, quarter):
            tr[s, q:q + quarter, :] = lax.dot_general(
                fac[s, q:q + quarter, :], reduced, (((1,), (1,)), ((), ())),
                preferred_element_type=F32,
            )
        for t in range(tile):
            parts[t, s * slots_one:(s + 1) * slots_one, :] = tr[
                s, pl.ds(t, slots_one, stride=tile), :
            ].astype(BF16)
        send_near(s)
    send_far(subs - 1)

    tail = None
    for k in range(mine):
        for s in range(subs):
            near_copies[s, k, 0].wait()
            far_copies[s, k].wait()
        kept[k] = (
            parts[here * mine + k].astype(F32) + near[k, 0].astype(F32) + far[k].astype(F32)
        ).astype(BF16)
        if main:
            send_faces(
                dot(place(main, 0, main), kept[k]), main_out.at[k], main_in.at[k], main_sem.at[k],
                main,
            )
        if extra:
            got = dot(place(extra, main, pad, k * (extra // mine)), kept[k])
            tail = got if k == 0 else tail + got
    if extra:
        send_faces(tail, tail_out, tail_in, tail_sem, extra)

    wide = coup[...].reshape(subs * inner_rows, order).astype(F32)
    filler = jnp.zeros((coup_t.shape[1] - subs * inner_rows, order), F32)
    coup_t[...] = jnp.concatenate([wide, filler], axis=0).T
    for t in range(tile):
        piece = coup_t[pl.ds(t, slots_one, stride=tile), :].T
        coup_out[t] = piece[:subs * inner_rows].astype(BF16)
    coup_in[here] = coup_out[pl.ds(here * mine, mine)]
    coup_copies = [
        remote(coup_out.at[pl.ds(b * mine, mine)], coup_in.at[here], coup_sem.at[i], {"blk": b})
        for i, b in enumerate((twin, cross, diag))
    ]
    for c in coup_copies:
        c.start()

    def own_side(value):
        return jnp.where(inside, 0.0, value.astype(F32))

    wait_faces(diag_out, diag_in, diag_sem, pad)
    divisors = own_side(diag_own[...]) + dot(collect(pad, 0, pad), diag_in[...])
    lane_t = lax.broadcasted_iota(jnp.int32, (slots, cols), 1)
    divisor = []
    for k in range(mine):
        one = jnp.sum(jnp.where(lane_t == here * mine + k, divisors, 0.0), axis=1, keepdims=True)
        divisor.append(jnp.where(live, one, 1.0))
    total = []
    for k in range(mine):
        both = own_side(kept[k])
        if main:
            wait_faces(main_out.at[k], main_in.at[k], main_sem.at[k], main)
            both += dot(collect(main, 0, main), main_in[k])
        total.append(both)
    if extra:
        every = jnp.concatenate(
            [collect(extra, main, pad, k * (extra // mine)) for k in range(mine)], axis=0
        )
        wait_faces(tail_out, tail_in, tail_sem, extra)
        rest = dot(every, tail_in[...])
        for k in range(mine):
            total[k] += rest[k * slots:(k + 1) * slots]
    for c in coup_copies:
        c.wait()
    coefs = [
        jnp.where(live, total[k] / divisor[k], 0.0).astype(BF16) for k in range(mine)
    ]
    for s in range(subs):
        left = [
            coup_in[:, k, s * inner_rows:(s + 1) * inner_rows, :].reshape(
                n_blk * inner_rows, slots_one
            )
            for k in range(mine)
        ]
        right = [coef[s * slots_one:(s + 1) * slots_one] for coef in coefs]
        got = dot(jnp.concatenate(left, axis=1), jnp.concatenate(right, axis=0))
        inner[:, s] = got.reshape(n_blk, inner_rows, cols)
    last = [
        remote(inner.at[b], out.at[here], last_sem.at[i], {"blk": b})
        for i, b in enumerate((twin, cross, diag))
    ]
    for c in last:
        c.start()
    stay = pltpu.make_async_copy(inner.at[here], out.at[here], local_sem.at[subs])
    stay.start()
    stay.wait()
    for c in last:
        c.wait()


def local(factor, samples, diagonal, coupling, blocks, peer_device, peer_lane, owns_face):
    n_sub, n_blk = lax.axis_size("sub"), lax.axis_size("blk")
    subs, order, quarter = factor.shape
    slots_one, tile = diagonal.shape[1], diagonal.shape[2]
    slots, cols = subs * slots_one, samples.shape[2]
    mine, inner_rows = tile // n_blk, coupling.shape[1]
    half_cycle = (n_sub - 1) // 2
    capacity = (FACE_HALF + half_cycle - 1) // half_cycle
    pad = -(-capacity // 16) * 16
    main = capacity // 16 * 16
    extra = -(-(capacity - main) * mine // 16) * 16
    flops = 4 * subs * order * quarter * cols
    hbm = pl.BlockSpec(memory_space=pltpu.HBM)
    sem = pltpu.SemaphoreType.DMA
    coup_lanes = -(-subs * inner_rows // 128) * 128

    def vmem(kind, *dims):
        return pltpu.VMEM(tuple(max(d, 1) for d in dims), kind)

    shares = pl.pallas_call(
        functools.partial(kernel, n_sub, n_blk, pad, main, extra),
        out_shape=jax.ShapeDtypeStruct((n_blk, subs, inner_rows, cols), F32),
        in_specs=[hbm] * 7,
        out_specs=hbm,
        scratch_shapes=[
            vmem(BF16, subs, order, quarter),
            vmem(BF16, n_blk, subs, quarter, cols),
            vmem(F32, subs, order, cols),
            vmem(BF16, tile, slots, cols),
            vmem(BF16, mine, 2, slots, cols),
            vmem(BF16, mine, slots, cols),
            vmem(BF16, mine, slots, cols),
            vmem(BF16, mine, slots, cols),
            vmem(BF16, n_sub * pad, cols),
            vmem(BF16, n_sub * pad, cols),
            vmem(BF16, mine, n_sub * main, cols),
            vmem(BF16, mine, n_sub * main, cols),
            vmem(BF16, n_sub * extra, cols),
            vmem(BF16, n_sub * extra, cols),
            vmem(F32, order, coup_lanes),
            vmem(BF16, tile, subs * inner_rows, slots_one),
            vmem(BF16, n_blk, mine, subs * inner_rows, slots_one),
            vmem(F32, n_blk, subs, inner_rows, cols),
            vmem(BF16, slots, cols),
            vmem(BF16, subs, tile, slots_one),
            vmem(BF16, *coupling.shape),
            vmem(jnp.int32, *peer_device.shape),
            vmem(jnp.int32, *peer_lane.shape),
            pltpu.SMEM(blocks.shape, jnp.int32),
            sem((subs + 1,)),
            sem((5,)),
            sem((subs, 2)),
            sem((subs, 2)),
            sem((subs, 2)),
            sem((subs, mine, 2, 2)),
            sem((subs, mine, 2)),
            sem((2,)),
            sem((mine, 2)),
            sem((2,)),
            sem((3, 2)),
            sem((3, 2)),
        ],
        compiler_params=pltpu.CompilerParams(
            collective_id=0, has_side_effects=True, vmem_limit_bytes=56 * 1024 * 1024
        ),
        cost_estimate=pl.CostEstimate(
            flops=flops, bytes_accessed=2 * factor.size, transcendentals=0
        ),
    )(factor, samples, jnp.swapaxes(diagonal, 1, 2), coupling, blocks, peer_device, peer_lane)
    return jnp.sum(shares, axis=0).astype(BF16)


def solution(mesh):
    placed = (
        P("sub", None, "blk"),
        P("sub", "blk", None),
        P("sub", None, None),
        P("sub", "blk", None),
        P("sub"),
        P("sub", None),
        P("sub", None),
        P("sub", None),
    )
    return jax.shard_map(
        local, mesh=mesh, in_specs=placed, out_specs=P("sub", "blk", None), check_vma=False
    )
```
